256 devices in a mesh: grp: 16 (over y_hi, x, core), dev: 16 (over y_lo, z).
Axes of the slice: x: 4, y: 4 (y_hi: 2, y_lo: 2; y = y_hi * 2 + y_lo), z: 8, core: 2. Of those that a mesh axis runs over, the one named last changes fastest.
Arguments:
- images: float32 [16384, 1152], P(('grp', 'dev')), may hold values from -0.2 to 0.2
- texts: float32 [16384, 1152], P(('grp', 'dev')), may hold values from -0.2 to 0.2
- log_temp: float32 [1], replicated, may hold values from 1.6 to 3
- bias: float32 [1], replicated, may hold values from -3 to -1
Outputs:
- grad_images: float32 [16384, 1152], P(('grp', 'dev'))
- grad_texts: float32 [16384, 1152], P(('grp', 'dev'))
The draws below stay inside these ranges and needn't reach their ends.
All inputs are finite; a program needn't handle non-finite values.
Results may differ from the reference program's by a relative error of at most 0.0063.
Values may be sent and summed in bfloat16 or wider, within the bound.
No kernel may reach another device: no remote copies, remote signals or barrier semaphores. Data moves between devices by JAX's collectives and lax.ppermute only.
A program may use at most 64 MiB of HBM per device.

```python
import jax
import jax.numpy as jnp
from jax import lax

D = 1152
ROWS = 64
PAIRS = 16384
N_GRP = 16
N_DEV = 16


def block_scale(key, shape, cuts, least, largest):
    factor_of, own = 1.0, jax.random.fold_in(key, 6)
    for dim, blocks in cuts:
        draws = jnp.exp(jax.random.uniform(jax.random.fold_in(own, dim), (blocks,), jnp.float32, least / len(cuts), largest / len(cuts)))
        factor_of = factor_of * jnp.repeat(draws, shape[dim] // blocks).reshape([-1 if axis == dim else 1 for axis in range(len(shape))])
    return factor_of


def bell_draw(rng, shape, scale, bound, shards=(), kind=jnp.bfloat16):
    array = jax.random.normal(rng, shape, jnp.float32) * scale
    if len(shards) > 0:
        array = block_scale(rng, shape, shards, -0.22, 0.18) * array
    return jnp.clip(array, min=-bound, max=bound).astype(kind)


def setup_inputs(seed: int = 0) -> dict:
    key_list = jax.random.split(jax.random.key(seed), 5)
    return {
        "images": bell_draw(key_list[0], (PAIRS, D), 0.03, 0.2, ((0, 256),), jnp.float32),
        "texts": bell_draw(key_list[1], (PAIRS, D), 0.03, 0.2, ((0, 256),), jnp.float32),
        "log_temp": jnp.clip(jax.random.uniform(key_list[2], (1,), jnp.float32, 1.6, 3.0), 1.6, 3.0),
        "bias": jnp.clip(jax.random.uniform(key_list[3], (1,), jnp.float32, -3.0, -1.0), -3.0, -1.0),
    }


def to_unit(raw):
    norm = jnp.sqrt(lax.optimization_barrier(jnp.sum(raw * raw, axis=1, keepdims=True)) + 1e-06)
    return (raw / norm, norm)

def from_unit(grad, unit, norm):
    return (grad - unit * lax.optimization_barrier(jnp.sum(unit * grad, axis=1, keepdims=True))) / norm

def rounded(value):
    return lax.optimization_barrier(value.astype(jnp.bfloat16)).astype(jnp.float32)

def reference(images, texts, log_temp, bias):
    temp = jnp.exp(log_temp[0])
    offset = bias[0]
    img_unit, img_norm = to_unit(images)
    txt_unit, txt_norm = to_unit(texts)
    xfull = rounded(img_unit)
    yfull = rounded(txt_unit)
    block = ROWS * N_DEV
    yblocks = yfull.reshape(N_GRP, block, D)
    row_ids = lax.broadcasted_iota(jnp.int32, (PAIRS, 1), 0)
    col_base = lax.broadcasted_iota(jnp.int32, (1, block), 1)

    def visit(dx, inputs):
        yblk, index = inputs
        dots = jnp.dot(xfull, yblk.T, precision=lax.Precision.HIGHEST)
        logits = temp * dots + offset
        cols = index * block + col_base
        delta = (row_ids == cols).astype(jnp.float32)
        coeff = rounded(jax.nn.sigmoid(logits) - delta)
        dx = dx + jnp.dot(coeff, yblk, precision=lax.Precision.HIGHEST)
        dy = jnp.dot(coeff.T, xfull, precision=lax.Precision.HIGHEST)
        return (dx, dy)
    indices = jnp.arange(N_GRP, dtype=jnp.int32)
    dx, dys = lax.scan(visit, jnp.zeros((PAIRS, D), jnp.float32), (yblocks, indices))
    dx = temp * dx
    dy = temp * dys.reshape(PAIRS, D)
    return (from_unit(dx, img_unit, img_norm), from_unit(dy, txt_unit, txt_norm))
```

```python
import jax
import jax.numpy as jnp
from jax import lax
from jax.experimental import pallas as pl
from jax.experimental.pallas import tpu as pltpu
from jax.sharding import Mesh, PartitionSpec as P

AXES = ("yh", "x", "core", "yl", "z")
PLANE = ("yh", "x", "yl")
BF = jnp.bfloat16
F32 = jnp.float32
NT = (((1,), (1,)), ((), ()))
TN = (((0,), (0,)), ((), ()))


def shifted(block, axis, distance):
    n = lax.axis_size(axis)
    return lax.ppermute(block, axis, [(i, (i + distance) % n) for i in range(n)])


def to_unit(raw):
    norm = jnp.sqrt(jnp.sum(raw * raw, axis=1, keepdims=True) + 1e-06)
    return (raw / norm, norm)


def from_unit(grad, unit, norm):
    return (grad - unit * jnp.sum(unit * grad, axis=1, keepdims=True)) / norm


def add(a, b):
    return (a.astype(F32) + b.astype(F32)).astype(BF)


def pair_kernel(place, scal, xs, xo, ts, dxs, dxo, dy, x, coeff):
    temp = scal[0]
    offset = scal[1]
    rows = 64
    half = xs.shape[0]
    pooled = ts.shape[0]
    x[0:half] = xs[...]
    x[half:] = xo[...]
    step = 256
    for j in range(pooled // step):
        sl = pl.ds(j * step, step)
        dots = lax.dot_general(ts[sl], x[...], NT, preferred_element_type=F32)
        coeff[sl] = jax.nn.sigmoid(temp * dots + offset).astype(BF)
    at = pl.multiple_of(place[0] * rows, rows)
    dots = lax.dot_general(ts[pl.ds(at, rows)], x[0:rows], NT, preferred_element_type=F32)
    eye = lax.broadcasted_iota(jnp.int32, (rows, rows), 0) == lax.broadcasted_iota(
        jnp.int32, (rows, rows), 1
    )
    own = jax.nn.sigmoid(temp * dots + offset) - eye.astype(F32)
    coeff[pl.ds(at, rows), 0:rows] = own.astype(BF)
    for i in range(half // step):
        part = lax.dot_general(
            coeff[:, half + i * step : half + (i + 1) * step], ts[...], TN, preferred_element_type=F32
        )
        dxo[pl.ds(i * step, step)] = part.astype(BF)
    for i in range(half // step):
        part = lax.dot_general(
            coeff[:, i * step : (i + 1) * step], ts[...], TN, preferred_element_type=F32
        )
        dxs[pl.ds(i * step, step)] = part
    for j in range(pooled // step):
        sl = pl.ds(j * step, step)
        dy[sl] = jnp.dot(coeff[sl], x[...], preferred_element_type=F32).astype(BF)


def pairs(place, scal, xs, xo, ts):
    half, width = xs.shape
    pooled = ts.shape[0]
    smem = pl.BlockSpec(memory_space=pltpu.SMEM)
    vmem = pl.BlockSpec(memory_space=pltpu.VMEM)
    return pl.pallas_call(
        pair_kernel,
        out_shape=(
            jax.ShapeDtypeStruct((half, width), F32),
            jax.ShapeDtypeStruct((half, width), BF),
            jax.ShapeDtypeStruct((pooled, width), BF),
        ),
        in_specs=[smem, smem, vmem, vmem, vmem],
        out_specs=(vmem, vmem, vmem),
        scratch_shapes=[
            pltpu.VMEM((2 * half, width), BF),
            pltpu.VMEM((pooled, 2 * half), BF),
        ],
        compiler_params=pltpu.CompilerParams(vmem_limit_bytes=48 * 2**20),
        cost_estimate=pl.CostEstimate(
            flops=6 * 2 * half * pooled * width, bytes_accessed=12 * 2**20, transcendentals=2 * half * pooled
        ),
    )(place, scal, xs, xo, ts)


def ring_gather(block):
    rows = block.shape[0]
    cut = rows // 2
    up = down = block
    held = [block]
    for _ in range(3):
        up = shifted(up, "z", 1)
        down = shifted(down, "z", -1)
        held += [up, down]
    far = jnp.concatenate([shifted(up[:cut], "z", 1), shifted(down[cut:], "z", -1)], 0)
    return jnp.concatenate(held + [far], 0)


def ring_reduce(parts):
    cut = parts.shape[1] // 2
    up = shifted(parts[7, :cut], "z", 1)
    down = shifted(parts[7, cut:], "z", -1)
    up = jnp.concatenate([add(parts[6, :cut], up), parts[6, cut:]], 0)
    down = jnp.concatenate([parts[5, :cut], add(parts[5, cut:], down)], 0)
    up, down = shifted(up, "z", 1), shifted(down, "z", -1)
    up, down = add(parts[4], up), add(parts[3], down)
    up, down = shifted(up, "z", 1), shifted(down, "z", -1)
    up, down = add(parts[2], up), add(parts[1], down)
    up, down = shifted(up, "z", 1), shifted(down, "z", -1)
    return parts[0].astype(F32) + up.astype(F32) + down.astype(F32)


def on_device(images, texts, log_temp, bias):
    temp = jnp.exp(log_temp[0])
    rows, width = images.shape
    img_unit, img_norm = to_unit(images)
    txt_unit, txt_norm = to_unit(texts)
    n_plane = lax.axis_size(PLANE)
    spread = jnp.broadcast_to(txt_unit.astype(BF)[None], (n_plane, rows, width))
    ts = lax.all_to_all(spread, PLANE, 0, 0, tiled=True).reshape(n_plane * rows, width)
    xs = ring_gather(img_unit.astype(BF))
    xo = shifted(xs, "core", 1)
    place = lax.axis_index(PLANE).astype(jnp.int32).reshape(1)
    scal = jnp.stack([temp, bias[0]])
    dxs, dxo, dy = pairs(place, scal, xs, xo, ts)
    dyr = lax.all_to_all(dy.reshape(n_plane, rows, width), PLANE, 0, 0, tiled=True)
    mine = add(dxs, shifted(dxo, "core", 1)).reshape(-1, rows, width)
    image_sum = ring_reduce(mine)
    text_sum = jnp.sum(dyr.astype(F32), axis=0)
    grad_images = from_unit(temp * image_sum, img_unit, img_norm)
    grad_texts = from_unit(temp * text_sum, txt_unit, txt_norm)
    return (grad_images, grad_texts)


def solution(mesh):
    fine = Mesh(mesh.devices.reshape(2, 4, 2, 2, 8), AXES)
    split = P(AXES, None)
    return jax.shard_map(
        on_device,
        mesh=fine,
        in_specs=(split, split, P(), P()),
        out_specs=(split, split),
        check_vma=False,
    )
```

```python
import jax
import jax.numpy as jnp
from jax import lax
from jax.experimental import pallas as pl
from jax.experimental.pallas import tpu as pltpu
from jax.sharding import Mesh, PartitionSpec as P

AXES = ("yh", "x", "core", "yl", "z")
PLANE = ("yh", "x", "yl")
BF = jnp.bfloat16
F32 = jnp.float32
ROWS = 64
NT = (((1,), (1,)), ((), ()))
TN = (((0,), (0,)), ((), ()))


def shifted(block, axis, distance):
    n = lax.axis_size(axis)
    return lax.ppermute(block, axis, [(i, (i + distance) % n) for i in range(n)])


def to_unit(raw):
    norm = jnp.sqrt(jnp.sum(raw * raw, axis=1, keepdims=True) + 1e-06)
    return (raw / norm, norm)


def from_unit(grad, unit, norm):
    return (grad - unit * jnp.sum(unit * grad, axis=1, keepdims=True)) / norm


def add(a, b):
    return (a.astype(F32) + b.astype(F32)).astype(BF)


def unit_rows(raw):
    norm = jnp.sqrt(jnp.sum(raw * raw, axis=1, keepdims=True) + 1e-06)
    return (raw / norm).astype(BF)


def spread_kernel(raw, out):
    unit = unit_rows(raw[...])
    for k in range(out.shape[0]):
        out[k] = unit


def unit_kernel(raw, out):
    out[...] = unit_rows(raw[...])


def coeff_kernel(place, scal, xs, xo, ts, dxo, coeff):
    temp = scal[0]
    offset = scal[1]
    rows = ROWS
    half = xs.shape[0]
    pooled = ts.shape[0]
    step = 256
    for j in range(pooled // step):
        sl = pl.ds(j * step, step)
        for h, x in ((0, xs), (half, xo)):
            dots = lax.dot_general(ts[sl], x[...], NT, preferred_element_type=F32)
            coeff[sl, h : h + half] = jax.nn.sigmoid(temp * dots + offset).astype(BF)
    at = pl.multiple_of(place[0] * rows, rows)
    dots = lax.dot_general(ts[pl.ds(at, rows)], xs[0:rows], NT, preferred_element_type=F32)
    eye = lax.broadcasted_iota(jnp.int32, (rows, rows), 0) == lax.broadcasted_iota(
        jnp.int32, (rows, rows), 1
    )
    own = jax.nn.sigmoid(temp * dots + offset) - eye.astype(F32)
    coeff[pl.ds(at, rows), 0:rows] = own.astype(BF)
    for i in range(half // step):
        cols = slice(half + i * step, half + (i + 1) * step)
        part = lax.dot_general(coeff[:, cols], ts[...], TN, preferred_element_type=F32)
        dxo[pl.ds(i * step, step)] = part.astype(BF)


def text_kernel(coeff, xs, xo, dy):
    half = xs.shape[0]
    step = 256
    for j in range(coeff.shape[0] // step):
        sl = pl.ds(j * step, step)
        part = jnp.dot(coeff[sl, 0:half], xs[...], preferred_element_type=F32)
        part += jnp.dot(coeff[sl, half:], xo[...], preferred_element_type=F32)
        dy[sl] = part.astype(BF)


def image_kernel(coeff, ts, other, dxs):
    step = 256
    for i in range(dxs.shape[0] // step):
        sl = pl.ds(i * step, step)
        part = lax.dot_general(coeff[:, i * step : (i + 1) * step], ts[...], TN, preferred_element_type=F32)
        dxs[sl] = (part + other[sl].astype(F32)).astype(BF)


def local(kernel, outs, args, smem=0, flops=0, nbytes=2**20, trans=0):
    specs = [pl.BlockSpec(memory_space=pltpu.SMEM)] * smem
    specs += [pl.BlockSpec(memory_space=pltpu.VMEM)] * (len(args) - smem)
    shapes = tuple(jax.ShapeDtypeStruct(shape, BF) for shape in outs)
    return pl.pallas_call(
        kernel,
        out_shape=shapes,
        in_specs=specs,
        out_specs=tuple(pl.BlockSpec(memory_space=pltpu.VMEM) for _ in outs),
        compiler_params=pltpu.CompilerParams(vmem_limit_bytes=40 * 2**20),
        cost_estimate=pl.CostEstimate(flops=flops, bytes_accessed=nbytes, transcendentals=trans),
    )(*args)


def ring_gather(block):
    up = down = block
    held = [block]
    for _ in range(3):
        up = shifted(up, "z", 1)
        down = shifted(down, "z", -1)
        held += [up, down]
    return jnp.concatenate(held + [shifted(up, "z", 1)], 0)


def ring_reduce(parts):
    up, down = shifted(parts[7], "z", 1), shifted(parts[5], "z", -1)
    up, down = shifted(add(parts[6], up), "z", 1), shifted(add(parts[3], down), "z", -1)
    up, down = shifted(add(parts[4], up), "z", 1), shifted(add(parts[1], down), "z", -1)
    up = shifted(add(parts[2], up), "z", 1)
    return parts[0].astype(F32) + up.astype(F32) + down.astype(F32)


def on_device(images, texts, log_temp, bias):
    temp = jnp.exp(log_temp[0])
    rows, width = images.shape
    n_plane = lax.axis_size(PLANE)
    half = ROWS * lax.axis_size("z")
    pooled = ROWS * n_plane
    (spread,) = local(spread_kernel, [(n_plane, rows, width)], [texts])
    spread, images = lax.optimization_barrier((spread, images))
    ts = lax.all_to_all(spread, PLANE, 0, 0, tiled=True).reshape(pooled, width)
    (x,) = local(unit_kernel, [(rows, width)], [images])
    xs = ring_gather(x)
    xo = shifted(xs, "core", 1)
    img_unit, img_norm = to_unit(images)
    txt_unit, txt_norm = to_unit(texts)
    place = lax.axis_index(PLANE).astype(jnp.int32).reshape(1)
    scal = jnp.stack([temp, bias[0]])
    unit_flops = 2 * half * pooled * width
    dxo, coeff = local(
        coeff_kernel, [(half, width), (pooled, 2 * half)], [place, scal, xs, xo, ts],
        smem=2, flops=3 * unit_flops, nbytes=8 * 2**20, trans=4 * half * pooled,
    )
    (dy,) = local(text_kernel, [(pooled, width)], [coeff, xs, xo], flops=2 * unit_flops, nbytes=7 * 2**20)
    dyr = lax.all_to_all(dy.reshape(n_plane, rows, width), PLANE, 0, 0, tiled=True)
    other = shifted(dxo, "core", 1)
    (mine,) = local(image_kernel, [(half, width)], [coeff, ts, other], flops=unit_flops, nbytes=6 * 2**20)
    image_sum = ring_reduce(mine.reshape(-1, rows, width))
    text_sum = jnp.sum(dyr.astype(F32), axis=0)
    grad_images = from_unit(temp * image_sum, img_unit, img_norm)
    grad_texts = from_unit(temp * text_sum, txt_unit, txt_norm)
    return (grad_images, grad_texts)


def solution(mesh):
    fine = Mesh(mesh.devices.reshape(2, 4, 2, 2, 8), AXES)
    split = P(AXES, None)
    return jax.shard_map(
        on_device,
        mesh=fine,
        in_specs=(split, split, P(), P()),
        out_specs=(split, split),
        check_vma=False,
    )
```

```python
import jax
import jax.numpy as jnp
from jax import lax
from jax.experimental import pallas as pl
from jax.experimental.pallas import tpu as pltpu
from jax.sharding import Mesh, PartitionSpec as P

AXES = ("yh", "x", "core", "yl", "z")
PLANE = ("yh", "x", "yl")
BF = jnp.bfloat16
F32 = jnp.float32
ROWS = 64
NT = (((1,), (1,)), ((), ()))
TN = (((0,), (0,)), ((), ()))


def shifted(block, axis, distance):
    n = lax.axis_size(axis)
    return lax.ppermute(block, axis, [(i, (i + distance) % n) for i in range(n)])


def to_unit(raw):
    norm = jnp.sqrt(jnp.sum(raw * raw, axis=1, keepdims=True) + 1e-06)
    return (raw / norm, norm)


def from_unit(grad, unit, norm):
    return (grad - unit * jnp.sum(unit * grad, axis=1, keepdims=True)) / norm


def add(a, b):
    return (a.astype(F32) + b.astype(F32)).astype(BF)


def unit_rows(raw):
    norm = jnp.sqrt(jnp.sum(raw * raw, axis=1, keepdims=True) + 1e-06)
    return (raw / norm).astype(BF)


def spread_kernel(raw, out, unit, sems):
    unit[...] = unit_rows(raw[...])
    copies = [pltpu.make_async_copy(unit, out.at[k], sems.at[k]) for k in range(out.shape[0])]
    for copy in copies:
        copy.start()
    for copy in copies:
        copy.wait()


def unit_kernel(raw, out):
    out[...] = unit_rows(raw[...])


def text_kernel(place, scal, xs, xo, ts, coeff, dy, part, sems):
    temp = scal[0]
    offset = scal[1]
    half = xs.shape[0]
    pooled = ts.shape[0]
    step = pooled // sems.shape[0]
    for j in range(pooled // step):
        sl = pl.ds(j * step, step)
        for h, x in ((0, xs), (half, xo)):
            dots = lax.dot_general(ts[sl], x[...], NT, preferred_element_type=F32)
            coeff[sl, h : h + half] = jax.nn.sigmoid(temp * dots + offset).astype(BF)
    at = pl.multiple_of(place[0] * ROWS, ROWS)
    dots = lax.dot_general(ts[pl.ds(at, ROWS)], xs[0:ROWS], NT, preferred_element_type=F32)
    eye = lax.broadcasted_iota(jnp.int32, (ROWS, ROWS), 0) == lax.broadcasted_iota(
        jnp.int32, (ROWS, ROWS), 1
    )
    own = jax.nn.sigmoid(temp * dots + offset) - eye.astype(F32)
    coeff[pl.ds(at, ROWS), 0:ROWS] = own.astype(BF)
    copies = []
    for j in range(pooled // step):
        sl = pl.ds(j * step, step)
        dots = jnp.dot(coeff[sl, 0:half], xs[...], preferred_element_type=F32)
        dots += jnp.dot(coeff[sl, half:], xo[...], preferred_element_type=F32)
        part[sl] = dots.astype(BF)
        copies.append(pltpu.make_async_copy(part.at[sl], dy.at[sl], sems.at[j]))
        copies[-1].start()
    for copy in copies:
        copy.wait()


def other_kernel(coeff, ts, dxo):
    half = dxo.shape[0]
    step = 256
    for i in range(half // step):
        cols = slice(half + i * step, half + (i + 1) * step)
        part = lax.dot_general(coeff[:, cols], ts[...], TN, preferred_element_type=F32)
        dxo[pl.ds(i * step, step)] = part.astype(BF)


def image_kernel(coeff, ts, other, dxs):
    step = 256
    for i in range(dxs.shape[0] // step):
        sl = pl.ds(i * step, step)
        part = lax.dot_general(coeff[:, i * step : (i + 1) * step], ts[...], TN, preferred_element_type=F32)
        dxs[sl] = (part + other[sl].astype(F32)).astype(BF)


VMEM = pl.BlockSpec(memory_space=pltpu.VMEM)
SMEM = pl.BlockSpec(memory_space=pltpu.SMEM)
HBM = pl.BlockSpec(memory_space=pltpu.HBM)


def local(kernel, outs, args, smem=0, scratch=(), flops=0, nbytes=2**20, trans=0):
    return pl.pallas_call(
        kernel,
        out_shape=tuple(jax.ShapeDtypeStruct(shape, BF) for shape, _ in outs),
        in_specs=[SMEM] * smem + [VMEM] * (len(args) - smem),
        out_specs=tuple(spec for _, spec in outs),
        scratch_shapes=list(scratch),
        compiler_params=pltpu.CompilerParams(vmem_limit_bytes=40 * 2**20),
        cost_estimate=pl.CostEstimate(flops=flops, bytes_accessed=nbytes, transcendentals=trans),
    )(*args)


def ring_gather(block):
    up = down = block
    held = [block]
    for _ in range(3):
        up = shifted(up, "z", 1)
        down = shifted(down, "z", -1)
        held += [up, down]
    return jnp.concatenate(held + [shifted(up, "z", 1)], 0)


def ring_reduce(parts):
    up, down = shifted(parts[7], "z", 1), shifted(parts[5], "z", -1)
    up, down = shifted(add(parts[6], up), "z", 1), shifted(add(parts[3], down), "z", -1)
    up, down = shifted(add(parts[4], up), "z", 1), shifted(add(parts[1], down), "z", -1)
    up = shifted(add(parts[2], up), "z", 1)
    return parts[0].astype(F32) + up.astype(F32) + down.astype(F32)


def on_device(images, texts, log_temp, bias):
    temp = jnp.exp(log_temp[0])
    rows, width = images.shape
    n_plane = lax.axis_size(PLANE)
    half = ROWS * lax.axis_size("z")
    pooled = ROWS * n_plane
    (spread,) = local(
        spread_kernel, [((n_plane, rows, width), HBM)], [texts],
        scratch=[pltpu.VMEM((rows, width), BF), pltpu.SemaphoreType.DMA((n_plane,))],
    )
    spread, images = lax.optimization_barrier((spread, images))
    ts = lax.all_to_all(spread, PLANE, 0, 0, tiled=True).reshape(pooled, width)
    (x,) = local(unit_kernel, [((rows, width), VMEM)], [images])
    xs = ring_gather(x)
    xo = shifted(xs, "core", 1)
    img_unit, img_norm = to_unit(images)
    txt_unit, txt_norm = to_unit(texts)
    place = lax.axis_index(PLANE).astype(jnp.int32).reshape(1)
    scal = jnp.stack([temp, bias[0]])
    unit_flops = 2 * half * pooled * width
    coeff, dy = local(
        text_kernel, [((pooled, 2 * half), VMEM), ((pooled, width), HBM)], [place, scal, xs, xo, ts], smem=2,
        scratch=[pltpu.VMEM((pooled, width), BF), pltpu.SemaphoreType.DMA((4,))],
        flops=4 * unit_flops, nbytes=9 * 2**20, trans=4 * half * pooled,
    )
    dyr = lax.all_to_all(dy.reshape(n_plane, rows, width), PLANE, 0, 0, tiled=True)
    (dxo,) = local(other_kernel, [((half, width), VMEM)], [coeff, ts], flops=unit_flops, nbytes=5 * 2**20)
    other = shifted(dxo, "core", 1)
    (mine,) = local(image_kernel, [((half, width), VMEM)], [coeff, ts, other], flops=unit_flops, nbytes=6 * 2**20)
    image_sum = ring_reduce(mine.reshape(-1, rows, width))
    text_sum = jnp.sum(dyr.astype(F32), axis=0)
    grad_images = from_unit(temp * image_sum, img_unit, img_norm)
    grad_texts = from_unit(temp * text_sum, txt_unit, txt_norm)
    return (grad_images, grad_texts)


def solution(mesh):
    fine = Mesh(mesh.devices.reshape(2, 4, 2, 2, 8), AXES)
    split = P(AXES, None)
    return jax.shard_map(
        on_device,
        mesh=fine,
        in_specs=(split, split, P(), P()),
        out_specs=(split, split),
        check_vma=False,
    )
```

```python
import jax
import jax.numpy as jnp
from jax import lax
from jax.experimental import pallas as pl
from jax.experimental.pallas import tpu as pltpu
from jax.sharding import Mesh, PartitionSpec as P

AXES = ("yh", "x", "core", "yl", "z")
PLANE = ("yh", "x", "yl")
BF = jnp.bfloat16
F32 = jnp.float32
ROWS = 64
NT = (((1,), (1,)), ((), ()))
TN = (((0,), (0,)), ((), ()))


def shifted(block, axis, distance):
    n = lax.axis_size(axis)
    return lax.ppermute(block, axis, [(i, (i + distance) % n) for i in range(n)])


def to_unit(raw):
    norm = jnp.sqrt(jnp.sum(raw * raw, axis=1, keepdims=True) + 1e-06)
    return (raw / norm, norm)


def from_unit(grad, unit, norm):
    return (grad - unit * jnp.sum(unit * grad, axis=1, keepdims=True)) / norm


def unit_rows(raw):
    norm = jnp.sqrt(jnp.sum(raw * raw, axis=1, keepdims=True) + 1e-06)
    return (raw / norm).astype(BF)


def spread_kernel(raw, out):
    unit = unit_rows(raw[...])
    for k in range(out.shape[0]):
        out[k] = unit


def unit_kernel(raw, out):
    out[...] = unit_rows(raw[...])


def text_kernel(place, scal, xs, ts, coeff, dy, part, sems):
    temp = scal[0]
    offset = scal[1]
    pooled = ts.shape[0]
    step = pooled // sems.shape[0]
    for j in range(pooled // step):
        sl = pl.ds(j * step, step)
        dots = lax.dot_general(ts[sl], xs[...], NT, preferred_element_type=F32)
        coeff[sl] = jax.nn.sigmoid(temp * dots + offset).astype(BF)
    at = pl.multiple_of(place[0] * ROWS, ROWS)
    wide = pl.multiple_of(place[1] // 2 * 2 * ROWS, 2 * ROWS)
    dots = lax.dot_general(ts[pl.ds(at, ROWS)], xs[pl.ds(wide, 2 * ROWS)], NT, preferred_element_type=F32)
    row = lax.broadcasted_iota(jnp.int32, dots.shape, 0) + place[1] % 2 * ROWS
    eye = row == lax.broadcasted_iota(jnp.int32, dots.shape, 1)
    own = jax.nn.sigmoid(temp * dots + offset) - eye.astype(F32)
    coeff[pl.ds(at, ROWS), pl.ds(wide, 2 * ROWS)] = own.astype(BF)
    copies = []
    for j in range(pooled // step):
        sl = pl.ds(j * step, step)
        part[sl] = jnp.dot(coeff[sl], xs[...], preferred_element_type=F32).astype(BF)
        copies.append(pltpu.make_async_copy(part.at[sl], dy.at[sl], sems.at[j]))
        copies[-1].start()
    for copy in copies:
        copy.wait()


def other_kernel(place, coeff, ts, dxo):
    half = dxo.shape[0]
    cols = pl.ds(pl.multiple_of((1 - place[2]) * half, half), half)
    part = lax.dot_general(coeff[:, cols], ts[...], TN, preferred_element_type=F32)
    dxo[...] = part.astype(BF)


def image_kernel(place, coeff, ts, other, dxs):
    half = dxs.shape[0]
    cols = pl.ds(pl.multiple_of(place[2] * half, half), half)
    part = lax.dot_general(coeff[:, cols], ts[...], TN, preferred_element_type=F32)
    part = (part + other[...].astype(F32)).astype(BF)
    n = half // ROWS
    for k in range(n):
        at = pl.multiple_of((k + n - place[3]) % n * ROWS, ROWS)
        dxs[pl.ds(at, ROWS)] = part[k * ROWS : (k + 1) * ROWS]


VMEM = pl.BlockSpec(memory_space=pltpu.VMEM)
SMEM = pl.BlockSpec(memory_space=pltpu.SMEM)
HBM = pl.BlockSpec(memory_space=pltpu.HBM)


def local(kernel, outs, args, smem=0, scratch=(), flops=0, nbytes=2**20, trans=0):
    return pl.pallas_call(
        kernel,
        out_shape=tuple((pltpu.HBM if spec is HBM else jax.ShapeDtypeStruct)(shape, BF) for shape, spec in outs),
        in_specs=[SMEM] * smem + [VMEM] * (len(args) - smem),
        out_specs=tuple(spec for _, spec in outs),
        scratch_shapes=list(scratch),
        compiler_params=pltpu.CompilerParams(vmem_limit_bytes=40 * 2**20),
        cost_estimate=pl.CostEstimate(flops=flops, bytes_accessed=nbytes, transcendentals=trans),
    )(*args)


def direct_reduce(parts):
    total = parts[0].astype(F32)
    for got in [shifted(parts[k], "z", k) for k in (4, 3, 5, 2, 6, 1, 7)]:
        total = total + got.astype(F32)
    return total


def on_device(images, texts, log_temp, bias):
    temp = jnp.exp(log_temp[0])
    rows, width = images.shape
    n_plane = lax.axis_size(PLANE)
    half = ROWS * lax.axis_size("z")
    pooled = ROWS * n_plane
    (x,) = local(unit_kernel, [((rows, width), VMEM)], [images])
    (spread,) = local(spread_kernel, [((n_plane, rows, width), VMEM)], [texts])
    xs = lax.all_gather(x, ("core", "z"), axis=0, tiled=True)
    ts = lax.all_to_all(spread, PLANE, 0, 0, tiled=True).reshape(pooled, width)
    img_unit, img_norm = to_unit(images)
    txt_unit, txt_norm = to_unit(texts)
    place = jnp.stack([lax.axis_index(a).astype(jnp.int32) for a in (PLANE, ("core", "z"), "core", "z")])
    scal = jnp.stack([temp, bias[0]])
    unit_flops = 2 * half * pooled * width
    coeff, dy = local(
        text_kernel, [((pooled, 2 * half), VMEM), ((pooled, width), HBM)], [place, scal, xs, ts], smem=2,
        scratch=[pltpu.VMEM((pooled, width), BF), pltpu.SemaphoreType.DMA((4,))],
        flops=4 * unit_flops, nbytes=9 * 2**20, trans=4 * half * pooled,
    )
    dyr = lax.all_to_all(dy.reshape(n_plane, rows, width), PLANE, 0, 0, tiled=True)
    (dxo,) = local(
        other_kernel, [((half, width), VMEM)], [place, coeff, ts], smem=1, flops=unit_flops, nbytes=5 * 2**20
    )
    other = shifted(dxo, "core", 1)
    (mine,) = local(
        image_kernel, [((half, width), VMEM)], [place, coeff, ts, other], smem=1, flops=unit_flops, nbytes=6 * 2**20
    )
    image_sum = direct_reduce(mine.reshape(-1, rows, width))
    text_sum = jnp.sum(dyr.astype(F32), axis=0)
    grad_images = from_unit(temp * image_sum, img_unit, img_norm)
    grad_texts = from_unit(temp * text_sum, txt_unit, txt_norm)
    return (grad_images, grad_texts)


def solution(mesh):
    fine = Mesh(mesh.devices.reshape(2, 4, 2, 2, 8), AXES)
    split = P(AXES, None)
    return jax.shard_map(
        on_device,
        mesh=fine,
        in_specs=(split, split, P(), P()),
        out_specs=(split, split),
        check_vma=False,
    )
```

```python
import jax
import jax.numpy as jnp
from jax import lax
from jax.experimental import pallas as pl
from jax.experimental.pallas import tpu as pltpu
from jax.sharding import Mesh, PartitionSpec as P

AXES = ("yh", "x", "core", "yl", "z")
PLANE = ("yh", "x", "yl")
BF = jnp.bfloat16
F32 = jnp.float32
ROWS = 64
NT = (((1,), (1,)), ((), ()))
TN = (((0,), (0,)), ((), ()))


def shifted(block, axis, distance):
    n = lax.axis_size(axis)
    return lax.ppermute(block, axis, [(i, (i + distance) % n) for i in range(n)])


def to_unit(raw):
    norm = jnp.sqrt(jnp.sum(raw * raw, axis=1, keepdims=True) + 1e-06)
    return (raw / norm, norm)


def from_unit(grad, unit, norm):
    return (grad - unit * jnp.sum(unit * grad, axis=1, keepdims=True)) / norm


def unit_rows(raw):
    norm = jnp.sqrt(jnp.sum(raw * raw, axis=1, keepdims=True) + 1e-06)
    return (raw / norm).astype(BF)


def spread_kernel(raw, out, unit, sems):
    unit[...] = unit_rows(raw[...])
    copies = [pltpu.make_async_copy(unit, out.at[k], sems.at[k]) for k in range(out.shape[0])]
    for copy in copies:
        copy.start()
    for copy in copies:
        copy.wait()


def unit_kernel(raw, out):
    out[...] = unit_rows(raw[...])


def pack_kernel(*refs):
    for k, block in enumerate(refs[:-1]):
        refs[-1][k * ROWS : (k + 1) * ROWS] = block[...]


def pair_kernel(place, scal, xs, xo, ts, coeff, dxo, dy, part, sems):
    temp = scal[0]
    offset = scal[1]
    half = xs.shape[0]
    pooled = ts.shape[0]
    step = pooled // sems.shape[0]
    for j in range(pooled // step):
        sl = pl.ds(j * step, step)
        for h, x in ((0, xs), (half, xo)):
            dots = lax.dot_general(ts[sl], x[...], NT, preferred_element_type=F32)
            coeff[sl, h : h + half] = jax.nn.sigmoid(temp * dots + offset).astype(BF)
    at = pl.multiple_of(place[0] * ROWS, ROWS)
    dots = lax.dot_general(ts[pl.ds(at, ROWS)], xs[0:ROWS], NT, preferred_element_type=F32)
    eye = lax.broadcasted_iota(jnp.int32, (ROWS, ROWS), 0) == lax.broadcasted_iota(
        jnp.int32, (ROWS, ROWS), 1
    )
    own = jax.nn.sigmoid(temp * dots + offset) - eye.astype(F32)
    coeff[pl.ds(at, ROWS), 0:ROWS] = own.astype(BF)
    copies = []
    for j in range(pooled // step):
        sl = pl.ds(j * step, step)
        dots = jnp.dot(coeff[sl, 0:half], xs[...], preferred_element_type=F32)
        dots += jnp.dot(coeff[sl, half:], xo[...], preferred_element_type=F32)
        part[sl] = dots.astype(BF)
        copies.append(pltpu.make_async_copy(part.at[sl], dy.at[sl], sems.at[j]))
        copies[-1].start()
    for i in range(half // step):
        cols = slice(half + i * step, half + (i + 1) * step)
        dots = lax.dot_general(coeff[:, cols], ts[...], TN, preferred_element_type=F32)
        dxo[pl.ds(i * step, step)] = dots.astype(BF)
    for copy in copies:
        copy.wait()


def image_kernel(coeff, ts, other, dxs):
    step = 256
    for i in range(dxs.shape[0] // step):
        sl = pl.ds(i * step, step)
        part = lax.dot_general(coeff[:, i * step : (i + 1) * step], ts[...], TN, preferred_element_type=F32)
        dxs[sl] = (part + other[sl].astype(F32)).astype(BF)


VMEM = pl.BlockSpec(memory_space=pltpu.VMEM)
SMEM = pl.BlockSpec(memory_space=pltpu.SMEM)
HBM = pl.BlockSpec(memory_space=pltpu.HBM)


def local(kernel, outs, args, smem=0, scratch=(), flops=0, nbytes=2**20, trans=0):
    return pl.pallas_call(
        kernel,
        out_shape=tuple((pltpu.HBM if spec is HBM else jax.ShapeDtypeStruct)(shape, BF) for shape, spec in outs),
        in_specs=[SMEM] * smem + [VMEM] * (len(args) - smem),
        out_specs=tuple(spec for _, spec in outs),
        scratch_shapes=list(scratch),
        compiler_params=pltpu.CompilerParams(vmem_limit_bytes=24 * 2**20),
        cost_estimate=pl.CostEstimate(flops=flops, bytes_accessed=nbytes, transcendentals=trans),
    )(*args)


PLACES = (4, 3, 5, 2, 6, 1, 7)


def direct_gather(block):
    return [block] + [shifted(block, "z", -k) for k in PLACES]


def direct_reduce(parts):
    total = parts[0].astype(F32)
    for got in [shifted(parts[i + 1], "z", k) for i, k in enumerate(PLACES)]:
        total = total + got.astype(F32)
    return total


def on_device(images, texts, log_temp, bias):
    temp = jnp.exp(log_temp[0])
    rows, width = images.shape
    n_plane = lax.axis_size(PLANE)
    half = ROWS * lax.axis_size("z")
    pooled = ROWS * n_plane
    (spread,) = local(
        spread_kernel, [((n_plane, rows, width), HBM)], [texts],
        scratch=[pltpu.VMEM((rows, width), BF), pltpu.SemaphoreType.DMA((n_plane,))],
    )
    spread, images = lax.optimization_barrier((spread, images))
    ts = lax.all_to_all(spread, PLANE, 0, 0, tiled=True).reshape(pooled, width)
    (x,) = local(unit_kernel, [((rows, width), VMEM)], [images])
    (xs,) = local(pack_kernel, [((half, width), VMEM)], direct_gather(x))
    xo = shifted(xs, "core", 1)
    img_unit, img_norm = to_unit(images)
    txt_unit, txt_norm = to_unit(texts)
    place = lax.axis_index(PLANE).astype(jnp.int32).reshape(1)
    scal = jnp.stack([temp, bias[0]])
    unit_flops = 2 * half * pooled * width
    coeff, dxo, dy = local(
        pair_kernel, [((pooled, 2 * half), VMEM), ((half, width), VMEM), ((pooled, width), HBM)],
        [place, scal, xs, xo, ts], smem=2,
        scratch=[pltpu.VMEM((pooled, width), BF), pltpu.SemaphoreType.DMA((4,))],
        flops=5 * unit_flops, nbytes=9 * 2**20, trans=4 * half * pooled,
    )
    dyr = lax.all_to_all(dy.reshape(n_plane, rows, width), PLANE, 0, 0, tiled=True)
    other = shifted(dxo, "core", 1)
    (mine,) = local(image_kernel, [((half, width), VMEM)], [coeff, ts, other], flops=unit_flops, nbytes=6 * 2**20)
    image_sum = direct_reduce(mine.reshape(-1, rows, width))
    text_sum = jnp.sum(dyr.astype(F32), axis=0)
    grad_images = from_unit(temp * image_sum, img_unit, img_norm)
    grad_texts = from_unit(temp * text_sum, txt_unit, txt_norm)
    return (grad_images, grad_texts)


def solution(mesh):
    fine = Mesh(mesh.devices.reshape(2, 4, 2, 2, 8), AXES)
    split = P(AXES, None)
    return jax.shard_map(
        on_device,
        mesh=fine,
        in_specs=(split, split, P(), P()),
        out_specs=(split, split),
        check_vma=False,
    )
```

```python
import jax
import jax.numpy as jnp
from jax import lax
from jax.experimental import pallas as pl
from jax.experimental.pallas import tpu as pltpu
from jax.sharding import Mesh, PartitionSpec as P

AXES = ("yh", "x", "core", "yl", "z")
PLANE = ("yh", "x", "yl")
BF = jnp.bfloat16
F32 = jnp.float32
LOG2E = 1.4426950408889634
ROWS = 64
NT = (((1,), (1,)), ((), ()))
TN = (((0,), (0,)), ((), ()))


def shifted(block, axis, distance):
    n = lax.axis_size(axis)
    return lax.ppermute(block, axis, [(i, (i + distance) % n) for i in range(n)])


def to_unit(raw):
    norm = jnp.sqrt(jnp.sum(raw * raw, axis=1, keepdims=True) + 1e-06)
    return (raw / norm, norm)


def from_unit(grad, unit, norm):
    return (grad - unit * jnp.sum(unit * grad, axis=1, keepdims=True)) / norm


def unit_rows(raw):
    norm = jnp.sqrt(jnp.sum(raw * raw, axis=1, keepdims=True) + 1e-06)
    return (raw / norm).astype(BF)


def spread_kernel(raw, out, unit, sems):
    unit[...] = unit_rows(raw[...])
    copies = [pltpu.make_async_copy(unit, out.at[k], sems.at[k]) for k in range(out.shape[0])]
    for copy in copies:
        copy.start()
    for copy in copies:
        copy.wait()


def unit_kernel(raw, out):
    out[...] = unit_rows(raw[...])


def pack_kernel(*refs):
    for k, block in enumerate(refs[:-1]):
        refs[-1][k * ROWS : (k + 1) * ROWS] = block[...]


def sigmoid(temp, offset, dots):
    return 1.0 / (1.0 + jnp.exp2(dots * (temp * -LOG2E) + offset * -LOG2E))


def pair_kernel(place, scal, xs, xo, ts, coeff, dxo, dy, x, held, part, sems):
    temp = scal[0]
    offset = scal[1]
    half = xs.shape[0]
    pooled = ts.shape[0]
    steps = 4
    step = pooled // steps
    loads = [
        pltpu.make_async_copy(xs, x.at[0:half], sems.at[0]),
        pltpu.make_async_copy(xo, x.at[half : 2 * half], sems.at[1]),
    ]
    for copy in loads:
        copy.start()
    for copy in loads:
        copy.wait()
    for j in range(steps):
        sl = pl.ds(j * step, step)
        dots = lax.dot_general(ts[sl], x[...], NT, preferred_element_type=F32)
        held[sl] = sigmoid(temp, offset, dots).astype(BF)
    at = pl.multiple_of(place[0] * ROWS, ROWS)
    dots = lax.dot_general(ts[pl.ds(at, ROWS)], x[0:ROWS], NT, preferred_element_type=F32)
    eye = lax.broadcasted_iota(jnp.int32, (ROWS, ROWS), 0) == lax.broadcasted_iota(
        jnp.int32, (ROWS, ROWS), 1
    )
    held[pl.ds(at, ROWS), 0:ROWS] = (sigmoid(temp, offset, dots) - eye.astype(F32)).astype(BF)
    copies = [pltpu.make_async_copy(held, coeff, sems.at[2])]
    copies[0].start()
    for j in range(steps):
        sl = pl.ds(j * step, step)
        part[sl] = jnp.dot(held[sl], x[...], preferred_element_type=F32).astype(BF)
        copies.append(pltpu.make_async_copy(part.at[sl], dy.at[sl], sems.at[3 + j]))
        copies[-1].start()
    wide = 256
    for i in range(half // wide):
        cols = slice(half + i * wide, half + (i + 1) * wide)
        dots = lax.dot_general(held[:, cols], ts[...], TN, preferred_element_type=F32)
        dxo[pl.ds(i * wide, wide)] = dots.astype(BF)
    for copy in copies:
        copy.wait()


def image_kernel(coeff, ts, other, *outs):
    wide = 256
    for i in range(other.shape[0] // wide):
        sl = pl.ds(i * wide, wide)
        part = lax.dot_general(coeff[:, i * wide : (i + 1) * wide], ts[...], TN, preferred_element_type=F32)
        part += other[sl].astype(F32)
        for k in range(wide // ROWS):
            out = outs[i * (wide // ROWS) + k]
            out[...] = part[k * ROWS : (k + 1) * ROWS].astype(out.dtype)


def text_kernel(scal, raw, got, out):
    total = got[0].astype(F32)
    for k in range(1, got.shape[0]):
        total += got[k].astype(F32)
    unit, norm = to_unit(raw[...])
    out[...] = from_unit(scal[0] * total, unit, norm)


VMEM = pl.BlockSpec(memory_space=pltpu.VMEM)
SMEM = pl.BlockSpec(memory_space=pltpu.SMEM)
HBM = pl.BlockSpec(memory_space=pltpu.HBM)


def local(kernel, outs, args, smem=0, hbm=0, scratch=(), flops=0, nbytes=2**20, trans=0, vmem=8):
    specs = [SMEM] * smem + [HBM] * hbm
    return pl.pallas_call(
        kernel,
        out_shape=tuple((pltpu.HBM if spec is HBM else jax.ShapeDtypeStruct)(shape, dtype) for shape, dtype, spec in outs),
        in_specs=specs + [VMEM] * (len(args) - len(specs)),
        out_specs=tuple(spec for _, _, spec in outs),
        scratch_shapes=list(scratch),
        compiler_params=pltpu.CompilerParams(vmem_limit_bytes=vmem * 2**20),
        cost_estimate=pl.CostEstimate(flops=flops, bytes_accessed=nbytes, transcendentals=trans),
    )(*args)


def add(a, b):
    return (a.astype(F32) + b.astype(F32)).astype(BF)


def ring_gather(block):
    far = shifted(block, "z", 4)
    up = [block]
    down = [block]
    for _ in range(3):
        up.append(shifted(up[-1], "z", -1))
        down.append(shifted(down[-1], "z", 1))
    return up + [far] + down[:0:-1]


def ring_reduce(parts):
    far = shifted(parts[4], "z", 4)
    up, down = parts[3], parts[5]
    for k in (2, 1, 0):
        up, down = shifted(up, "z", 1), shifted(down, "z", -1)
        if k:
            up, down = add(parts[k], up), add(parts[8 - k], down)
    return parts[0] + up.astype(F32) + down.astype(F32) + far.astype(F32)


def on_device(images, texts, log_temp, bias):
    temp = jnp.exp(log_temp[0])
    rows, width = images.shape
    n_plane = lax.axis_size(PLANE)
    half = ROWS * lax.axis_size("z")
    pooled = ROWS * n_plane
    (spread,) = local(
        spread_kernel, [((n_plane, rows, width), BF, HBM)], [texts],
        scratch=[pltpu.VMEM((rows, width), BF), pltpu.SemaphoreType.DMA((n_plane,))],
    )
    spread, images = lax.optimization_barrier((spread, images))
    ts = lax.all_to_all(spread, PLANE, 0, 0, tiled=True).reshape(pooled, width)
    (x,) = local(unit_kernel, [((rows, width), BF, VMEM)], [images])
    (xs,) = local(pack_kernel, [((half, width), BF, VMEM)], ring_gather(x))
    xo = shifted(xs, "core", 1)
    img_unit, img_norm = to_unit(images)
    place = lax.axis_index(PLANE).astype(jnp.int32).reshape(1)
    scal = jnp.stack([temp, bias[0]])
    unit_flops = 2 * half * pooled * width
    coeff, dxo, dy = local(
        pair_kernel,
        [((pooled, 2 * half), BF, HBM), ((half, width), BF, VMEM), ((pooled, width), BF, HBM)],
        [place, scal, xs, xo, ts], smem=2, hbm=2,
        scratch=[
            pltpu.VMEM((2 * half, width), BF),
            pltpu.VMEM((pooled, 2 * half), BF),
            pltpu.VMEM((pooled, width), BF),
            pltpu.SemaphoreType.DMA((7,)),
        ],
        flops=5 * unit_flops, nbytes=9 * 2**20, trans=4 * half * pooled, vmem=24,
    )
    dyr = lax.all_to_all(dy.reshape(n_plane, rows, width), PLANE, 0, 0, tiled=True)
    other = shifted(dxo, "core", 1)
    parts = local(
        image_kernel,
        [((rows, width), BF if k else F32, VMEM) for k in range(half // rows)],
        [coeff, ts, other], vmem=16,
    )
    image_sum = ring_reduce(parts)
    grad_images = from_unit(temp * image_sum, img_unit, img_norm)
    (grad_texts,) = local(text_kernel, [((rows, width), F32, VMEM)], [scal, texts, dyr], smem=1, vmem=8)
    return (grad_images, grad_texts)


def solution(mesh):
    fine = Mesh(mesh.devices.reshape(2, 4, 2, 2, 8), AXES)
    split = P(AXES, None)
    return jax.shard_map(
        on_device,
        mesh=fine,
        in_specs=(split, split, P(), P()),
        out_specs=(split, split),
        check_vma=False,
    )
```

```python
import jax
import jax.numpy as jnp
from jax import lax
from jax.experimental import pallas as pl
from jax.experimental.pallas import tpu as pltpu
from jax.sharding import Mesh, PartitionSpec as P

AXES = ("yh", "x", "core", "yl", "z")
PLANE = ("yh", "x", "yl")
BF = jnp.bfloat16
F32 = jnp.float32
LOG2E = 1.4426950408889634
ROWS = 64
NT = (((1,), (1,)), ((), ()))
TN = (((0,), (0,)), ((), ()))


def shifted(block, axis, distance):
    n = lax.axis_size(axis)
    return lax.ppermute(block, axis, [(i, (i + distance) % n) for i in range(n)])


def to_unit(raw):
    norm = jnp.sqrt(jnp.sum(raw * raw, axis=1, keepdims=True) + 1e-06)
    return (raw / norm, norm)


def from_unit(grad, unit, norm):
    return (grad - unit * jnp.sum(unit * grad, axis=1, keepdims=True)) / norm


def unit_rows(raw):
    norm = jnp.sqrt(jnp.sum(raw * raw, axis=1, keepdims=True) + 1e-06)
    return (raw / norm).astype(BF)


def spread_kernel(raw, out, unit, sems):
    unit[...] = unit_rows(raw[...])
    copies = [pltpu.make_async_copy(unit, out.at[k], sems.at[k]) for k in range(out.shape[0])]
    for copy in copies:
        copy.start()
    for copy in copies:
        copy.wait()


def unit_kernel(raw, out):
    out[...] = unit_rows(raw[...])


def pack_kernel(*refs):
    for k, block in enumerate(refs[:-1]):
        refs[-1][k * ROWS : (k + 1) * ROWS] = block[...]


def sigmoid(temp, offset, dots):
    return 1.0 / (1.0 + jnp.exp2(dots * (temp * -LOG2E) + offset * -LOG2E))


def pair_kernel(place, scal, xs, xo, ts, coeff, dxo, dy, x, held, part, sems):
    temp = scal[0]
    offset = scal[1]
    half = xs.shape[0]
    pooled = ts.shape[0]
    steps = 4
    step = pooled // steps
    loads = [
        pltpu.make_async_copy(xs, x.at[0:half], sems.at[0]),
        pltpu.make_async_copy(xo, x.at[half : 2 * half], sems.at[1]),
    ]
    for copy in loads:
        copy.start()
    for copy in loads:
        copy.wait()
    for j in range(steps):
        sl = pl.ds(j * step, step)
        dots = lax.dot_general(ts[sl], x[...], NT, preferred_element_type=F32)
        held[sl] = sigmoid(temp, offset, dots).astype(BF)
    at = pl.multiple_of(place[0] * ROWS, ROWS)
    dots = lax.dot_general(ts[pl.ds(at, ROWS)], x[0:ROWS], NT, preferred_element_type=F32)
    eye = lax.broadcasted_iota(jnp.int32, (ROWS, ROWS), 0) == lax.broadcasted_iota(
        jnp.int32, (ROWS, ROWS), 1
    )
    held[pl.ds(at, ROWS), 0:ROWS] = (sigmoid(temp, offset, dots) - eye.astype(F32)).astype(BF)
    copies = [pltpu.make_async_copy(held, coeff, sems.at[2])]
    copies[0].start()
    for j in range(steps):
        sl = pl.ds(j * step, step)
        part[sl] = jnp.dot(held[sl], x[...], preferred_element_type=F32).astype(BF)
        copies.append(pltpu.make_async_copy(part.at[sl], dy.at[sl], sems.at[3 + j]))
        copies[-1].start()
    wide = 256
    for i in range(half // wide):
        cols = slice(half + i * wide, half + (i + 1) * wide)
        dots = lax.dot_general(held[:, cols], ts[...], TN, preferred_element_type=F32)
        dxo[pl.ds(i * wide, wide)] = dots.astype(BF)
    for copy in copies:
        copy.wait()


def image_kernel(coeff, ts, other, own, rest, held, sems):
    wide = 256
    n = other.shape[0] // wide
    loads = []
    for i in range(n):
        cols = slice(i * wide, (i + 1) * wide)
        loads.append(pltpu.make_async_copy(coeff.at[:, cols], held.at[:, cols], sems.at[i]))
        loads[-1].start()
    for i in range(n):
        loads[i].wait()
        part = lax.dot_general(held[:, i * wide : (i + 1) * wide], ts[...], TN, preferred_element_type=F32)
        part += other[pl.ds(i * wide, wide)].astype(F32)
        if i == 0:
            own[...] = part[0:ROWS]
            rest[0 : wide - ROWS] = part[ROWS:].astype(BF)
        else:
            rest[pl.ds(i * wide - ROWS, wide)] = part.astype(BF)


def text_kernel(scal, raw, got, out):
    total = got[0].astype(F32)
    for k in range(1, got.shape[0]):
        total += got[k].astype(F32)
    unit, norm = to_unit(raw[...])
    out[...] = from_unit(scal[0] * total, unit, norm)


VMEM = pl.BlockSpec(memory_space=pltpu.VMEM)
SMEM = pl.BlockSpec(memory_space=pltpu.SMEM)
HBM = pl.BlockSpec(memory_space=pltpu.HBM)


def local(kernel, outs, args, smem=0, hbm=0, scratch=(), flops=0, nbytes=2**20, trans=0, vmem=8):
    specs = [SMEM] * smem + [HBM] * hbm
    return pl.pallas_call(
        kernel,
        out_shape=tuple((pltpu.HBM if spec is HBM else jax.ShapeDtypeStruct)(shape, dtype) for shape, dtype, spec in outs),
        in_specs=specs + [VMEM] * (len(args) - len(specs)),
        out_specs=tuple(spec for _, _, spec in outs),
        scratch_shapes=list(scratch),
        compiler_params=pltpu.CompilerParams(vmem_limit_bytes=vmem * 2**20),
        cost_estimate=pl.CostEstimate(flops=flops, bytes_accessed=nbytes, transcendentals=trans),
    )(*args)


def add(a, b):
    return (a.astype(F32) + b.astype(F32)).astype(BF)


def ring_gather(block):
    far = shifted(block, "z", 4)
    up = [block]
    down = [block]
    for _ in range(3):
        up.append(shifted(up[-1], "z", -1))
        down.append(shifted(down[-1], "z", 1))
    return up + [far] + down[:0:-1]


def near_reduce(own, rest):
    direct = [shifted(rest[k - 1], "z", k) for k in (4, 3, 5)]
    up, down = shifted(rest[1], "z", 1), shifted(rest[5], "z", -1)
    up, down = shifted(add(rest[0], up), "z", 1), shifted(add(rest[6], down), "z", -1)
    for got in direct + [up, down]:
        own = own + got.astype(F32)
    return own


def on_device(images, texts, log_temp, bias):
    temp = jnp.exp(log_temp[0])
    rows, width = images.shape
    n_plane = lax.axis_size(PLANE)
    half = ROWS * lax.axis_size("z")
    pooled = ROWS * n_plane
    (spread,) = local(
        spread_kernel, [((n_plane, rows, width), BF, HBM)], [texts],
        scratch=[pltpu.VMEM((rows, width), BF), pltpu.SemaphoreType.DMA((n_plane,))],
    )
    spread, images = lax.optimization_barrier((spread, images))
    ts = lax.all_to_all(spread, PLANE, 0, 0, tiled=True).reshape(pooled, width)
    (x,) = local(unit_kernel, [((rows, width), BF, VMEM)], [images])
    (xs,) = local(pack_kernel, [((half, width), BF, VMEM)], ring_gather(x))
    xo = shifted(xs, "core", 1)
    img_unit, img_norm = to_unit(images)
    place = lax.axis_index(PLANE).astype(jnp.int32).reshape(1)
    scal = jnp.stack([temp, bias[0]])
    unit_flops = 2 * half * pooled * width
    coeff, dxo, dy = local(
        pair_kernel,
        [((pooled, 2 * half), BF, HBM), ((half, width), BF, VMEM), ((pooled, width), BF, HBM)],
        [place, scal, xs, xo, ts], smem=2, hbm=2,
        scratch=[
            pltpu.VMEM((2 * half, width), BF),
            pltpu.VMEM((pooled, 2 * half), BF),
            pltpu.VMEM((pooled, width), BF),
            pltpu.SemaphoreType.DMA((7,)),
        ],
        flops=5 * unit_flops, nbytes=9 * 2**20, trans=4 * half * pooled, vmem=24,
    )
    dyr = lax.all_to_all(dy.reshape(n_plane, rows, width), PLANE, 0, 0, tiled=True)
    other = shifted(dxo, "core", 1)
    own, rest = local(
        image_kernel,
        [((rows, width), F32, VMEM), ((half - rows, width), BF, VMEM)],
        [coeff, ts, other], hbm=1, vmem=16, flops=unit_flops, nbytes=6 * 2**20,
        scratch=[pltpu.VMEM((pooled, half), BF), pltpu.SemaphoreType.DMA((half // 256,))],
    )
    image_sum = near_reduce(own, rest.reshape(-1, rows, width))
    grad_images = from_unit(temp * image_sum, img_unit, img_norm)
    (grad_texts,) = local(text_kernel, [((rows, width), F32, VMEM)], [scal, texts, dyr], smem=1, vmem=8)
    return (grad_images, grad_texts)


def solution(mesh):
    fine = Mesh(mesh.devices.reshape(2, 4, 2, 2, 8), AXES)
    split = P(AXES, None)
    return jax.shard_map(
        on_device,
        mesh=fine,
        in_specs=(split, split, P(), P()),
        out_specs=(split, split),
        check_vma=False,
    )
```

```python
import jax
import jax.numpy as jnp
from jax import lax
from jax.experimental import pallas as pl
from jax.experimental.pallas import tpu as pltpu
from jax.sharding import Mesh, PartitionSpec as P

AXES = ("yh", "x", "core", "yl", "z")
PLANE = ("yh", "x", "yl")
BF = jnp.bfloat16
F32 = jnp.float32
LOG2E = 1.4426950408889634
ROWS = 64
NT = (((1,), (1,)), ((), ()))
TN = (((0,), (0,)), ((), ()))


def shifted(block, axis, distance):
    n = lax.axis_size(axis)
    return lax.ppermute(block, axis, [(i, (i + distance) % n) for i in range(n)])


def to_unit(raw):
    norm = jnp.sqrt(jnp.sum(raw * raw, axis=1, keepdims=True) + 1e-06)
    return (raw / norm, norm)


def from_unit(grad, unit, norm):
    return (grad - unit * jnp.sum(unit * grad, axis=1, keepdims=True)) / norm


def unit_rows(raw):
    norm = jnp.sqrt(jnp.sum(raw * raw, axis=1, keepdims=True) + 1e-06)
    return (raw / norm).astype(BF)


def spread_kernel(raw, out, unit, sems):
    unit[...] = unit_rows(raw[...])
    copies = [pltpu.make_async_copy(unit, out.at[k], sems.at[k]) for k in range(out.shape[0])]
    for copy in copies:
        copy.start()
    for copy in copies:
        copy.wait()


def unit_kernel(raw, out):
    out[...] = unit_rows(raw[...])


def pack_kernel(*refs):
    for k, block in enumerate(refs[:-1]):
        refs[-1][k * ROWS : (k + 1) * ROWS] = block[...]


def sigmoid(temp, offset, dots):
    return 1.0 / (1.0 + jnp.exp2(dots * (temp * -LOG2E) + offset * -LOG2E))


def pair_kernel(place, scal, xs, xo, ts, dxs, dxo, dy, x, held, mine, theirs, part, sems):
    temp = scal[0]
    offset = scal[1]
    half = xs.shape[0]
    pooled = ts.shape[0]
    wide = 512
    step = 256
    loads = [
        pltpu.make_async_copy(xs, x.at[0:half], sems.at[0]),
        pltpu.make_async_copy(xo, x.at[half : 2 * half], sems.at[1]),
    ]
    for copy in loads:
        copy.start()
    for h, copy in enumerate(loads):
        copy.wait()
        cols = slice(h * half, (h + 1) * half)
        for j in range(pooled // step):
            sl = pl.ds(j * step, step)
            dots = lax.dot_general(ts[sl], x[cols], NT, preferred_element_type=F32)
            held[sl, cols] = sigmoid(temp, offset, dots).astype(BF)
    at = pl.multiple_of(place[0] * ROWS, ROWS)
    dots = lax.dot_general(ts[pl.ds(at, ROWS)], x[0:ROWS], NT, preferred_element_type=F32)
    eye = lax.broadcasted_iota(jnp.int32, (ROWS, ROWS), 0) == lax.broadcasted_iota(
        jnp.int32, (ROWS, ROWS), 1
    )
    held[pl.ds(at, ROWS), 0:ROWS] = (sigmoid(temp, offset, dots) - eye.astype(F32)).astype(BF)
    copies = []

    def send(src, dst):
        copies.append(pltpu.make_async_copy(src, dst, sems.at[2 + len(copies)]))
        copies[-1].start()

    for h, (buf, out) in enumerate(((mine, dxs), (theirs, dxo))):
        for i in range(0, half, wide):
            cols = slice(h * half + i, h * half + i + wide)
            dots = lax.dot_general(held[:, cols], ts[...], TN, preferred_element_type=F32)
            buf[i : i + wide] = dots.astype(buf.dtype)
            send(buf.at[i : i + wide], out.at[i : i + wide])
    for j in range(0, pooled, step):
        part[j : j + step] = jnp.dot(held[j : j + step], x[...], preferred_element_type=F32).astype(BF)
        send(part.at[j : j + step], dy.at[j : j + step])
    for copy in copies:
        copy.wait()


def join_kernel(dxs, other, own, rest):
    own[...] = dxs[0:ROWS] + other[0:ROWS].astype(F32)
    rest[...] = (dxs[ROWS:] + other[ROWS:].astype(F32)).astype(BF)


def finish_kernel(scal, images, texts, dyr, own, *refs):
    got, (out_images, out_texts) = refs[:-2], refs[-2:]
    total = dyr[0].astype(F32)
    for k in range(1, dyr.shape[0]):
        total += dyr[k].astype(F32)
    unit, norm = to_unit(texts[...])
    out_texts[...] = from_unit(scal[0] * total, unit, norm)
    total = own[...]
    for part in got:
        total += part[...].astype(F32)
    unit, norm = to_unit(images[...])
    out_images[...] = from_unit(scal[0] * total, unit, norm)


VMEM = pl.BlockSpec(memory_space=pltpu.VMEM)
SMEM = pl.BlockSpec(memory_space=pltpu.SMEM)
HBM = pl.BlockSpec(memory_space=pltpu.HBM)


def local(kernel, outs, args, smem=0, hbm=0, scratch=(), flops=0, nbytes=2**20, trans=0, vmem=8):
    specs = [SMEM] * smem + [HBM] * hbm
    return pl.pallas_call(
        kernel,
        out_shape=tuple((pltpu.HBM if spec is HBM else jax.ShapeDtypeStruct)(shape, dtype) for shape, dtype, spec in outs),
        in_specs=specs + [VMEM] * (len(args) - len(specs)),
        out_specs=tuple(spec for _, _, spec in outs),
        scratch_shapes=list(scratch),
        compiler_params=pltpu.CompilerParams(vmem_limit_bytes=vmem * 2**20),
        cost_estimate=pl.CostEstimate(flops=flops, bytes_accessed=nbytes, transcendentals=trans),
    )(*args)


def add(a, b):
    return (a.astype(F32) + b.astype(F32)).astype(BF)


def ring_gather(block):
    far = shifted(block, "z", 4)
    up = [block]
    down = [block]
    for _ in range(3):
        up.append(shifted(up[-1], "z", -1))
        down.append(shifted(down[-1], "z", 1))
    return up + [far] + down[:0:-1]


def near_reduce(rest):
    direct = [shifted(rest[k - 1], "z", k) for k in (4, 3, 5)]
    up, down = shifted(rest[1], "z", 1), shifted(rest[5], "z", -1)
    up, down = shifted(add(rest[0], up), "z", 1), shifted(add(rest[6], down), "z", -1)
    return direct + [up, down]


def on_device(images, texts, log_temp, bias):
    temp = jnp.exp(log_temp[0])
    rows, width = images.shape
    n_plane = lax.axis_size(PLANE)
    half = ROWS * lax.axis_size("z")
    pooled = ROWS * n_plane
    (spread,) = local(
        spread_kernel, [((n_plane, rows, width), BF, HBM)], [texts],
        scratch=[pltpu.VMEM((rows, width), BF), pltpu.SemaphoreType.DMA((n_plane,))],
    )
    spread, images = lax.optimization_barrier((spread, images))
    ts = lax.all_to_all(spread, PLANE, 0, 0, tiled=True).reshape(pooled, width)
    (x,) = local(unit_kernel, [((rows, width), BF, VMEM)], [images])
    (xs,) = local(pack_kernel, [((half, width), BF, VMEM)], ring_gather(x))
    xo = shifted(xs, "core", 1)
    place = lax.axis_index(PLANE).astype(jnp.int32).reshape(1)
    scal = jnp.stack([temp, bias[0]])
    unit_flops = 2 * half * pooled * width
    dxs, dxo, dy = local(
        pair_kernel,
        [((half, width), F32, HBM), ((half, width), BF, HBM), ((pooled, width), BF, HBM)],
        [place, scal, xs, xo, ts], smem=2, hbm=2,
        scratch=[
            pltpu.VMEM((2 * half, width), BF),
            pltpu.VMEM((pooled, 2 * half), BF),
            pltpu.VMEM((half, width), F32),
            pltpu.VMEM((half, width), BF),
            pltpu.VMEM((pooled, width), BF),
            pltpu.SemaphoreType.DMA((8,)),
        ],
        flops=6 * unit_flops, nbytes=9 * 2**20, trans=4 * half * pooled, vmem=24,
    )
    dyr = lax.all_to_all(dy.reshape(n_plane, rows, width), PLANE, 0, 0, tiled=True)
    other = shifted(dxo, "core", 1)
    own, rest = local(
        join_kernel, [((rows, width), F32, VMEM), ((half - rows, width), BF, VMEM)], [dxs, other],
        nbytes=5 * 2**20, vmem=16,
    )
    got = near_reduce(rest.reshape(-1, rows, width))
    grad_images, grad_texts = local(
        finish_kernel, [((rows, width), F32, VMEM)] * 2, [scal, images, texts, dyr, own] + got, smem=1, vmem=16
    )
    return (grad_images, grad_texts)


def solution(mesh):
    fine = Mesh(mesh.devices.reshape(2, 4, 2, 2, 8), AXES)
    split = P(AXES, None)
    return jax.shard_map(
        on_device,
        mesh=fine,
        in_specs=(split, split, P(), P()),
        out_specs=(split, split),
        check_vma=False,
    )
```

```python
import jax
import jax.numpy as jnp
import numpy as np
from jax import lax
from jax.experimental import pallas as pl
from jax.experimental.pallas import tpu as pltpu
from jax.sharding import Mesh, PartitionSpec as P

AXES = ("yh", "x", "core", "yl", "z")
PLANE = ("yh", "x", "yl")
BF = jnp.bfloat16
F32 = jnp.float32
LOG2E = 1.4426950408889634
ROWS = 64
NT = (((1,), (1,)), ((), ()))
TN = (((0,), (0,)), ((), ()))


def plane_groups():
    at = np.arange(256).reshape(2, 4, 2, 2, 8)
    along_x, along_y = [], []
    for core in range(2):
        along_x.append(at[:, :, core].transpose(0, 2, 3, 1).reshape(-1, 4).tolist())
        along_y.append(at[:, :, core].transpose(1, 3, 0, 2).reshape(-1, 4).tolist())
    whole = at[:, :, 0].transpose(3, 0, 2, 1).reshape(-1, 16).tolist()
    whole += at[:, :, 1].transpose(3, 1, 0, 2).reshape(-1, 16).tolist()
    outer = along_y[0] + along_x[1]
    inner = along_x[0] + along_y[1]
    return whole, outer, inner


WHOLE, OUTER, INNER = plane_groups()


def swapped(blocks, groups):
    return lax.all_to_all(blocks, AXES, 0, 0, axis_index_groups=groups, tiled=True)


def shifted(block, axis, distance):
    n = lax.axis_size(axis)
    return lax.ppermute(block, axis, [(i, (i + distance) % n) for i in range(n)])


def to_unit(raw):
    norm = jnp.sqrt(jnp.sum(raw * raw, axis=1, keepdims=True) + 1e-06)
    return (raw / norm, norm)


def from_unit(grad, unit, norm):
    return (grad - unit * jnp.sum(unit * grad, axis=1, keepdims=True)) / norm


def unit_rows(raw):
    norm = jnp.sqrt(jnp.sum(raw * raw, axis=1, keepdims=True) + 1e-06)
    return (raw / norm).astype(BF)


def spread_kernel(raw, out, unit, sems):
    unit[...] = unit_rows(raw[...])
    copies = [pltpu.make_async_copy(unit, out.at[k], sems.at[k]) for k in range(out.shape[0])]
    for copy in copies:
        copy.start()
    for copy in copies:
        copy.wait()


def unit_kernel(raw, out):
    out[...] = unit_rows(raw[...])


def pack_kernel(*refs):
    for k, block in enumerate(refs[:-1]):
        refs[-1][k * ROWS : (k + 1) * ROWS] = block[...]


def sigmoid(temp, offset, dots):
    return 1.0 / (1.0 + jnp.exp2(dots * (temp * -LOG2E) + offset * -LOG2E))


def pair_kernel(place, scal, xs, xo, ts, dxs, dxo, dy, x, held, mine, theirs, part, sems):
    temp = scal[0]
    offset = scal[1]
    half = xs.shape[0]
    pooled = ts.shape[0]
    wide = 512
    step = 256
    loads = [
        pltpu.make_async_copy(xs, x.at[0:half], sems.at[0]),
        pltpu.make_async_copy(xo, x.at[half : 2 * half], sems.at[1]),
    ]
    for copy in loads:
        copy.start()
    for h, copy in enumerate(loads):
        copy.wait()
        cols = slice(h * half, (h + 1) * half)
        for j in range(pooled // step):
            sl = pl.ds(j * step, step)
            dots = lax.dot_general(ts[sl], x[cols], NT, preferred_element_type=F32)
            held[sl, cols] = sigmoid(temp, offset, dots).astype(BF)
    at = pl.multiple_of(place[0] * ROWS, ROWS)
    dots = lax.dot_general(ts[pl.ds(at, ROWS)], x[0:ROWS], NT, preferred_element_type=F32)
    eye = lax.broadcasted_iota(jnp.int32, (ROWS, ROWS), 0) == lax.broadcasted_iota(
        jnp.int32, (ROWS, ROWS), 1
    )
    held[pl.ds(at, ROWS), 0:ROWS] = (sigmoid(temp, offset, dots) - eye.astype(F32)).astype(BF)
    copies = []

    def send(src, dst):
        copies.append(pltpu.make_async_copy(src, dst, sems.at[2 + len(copies)]))
        copies[-1].start()

    for h, (buf, out) in enumerate(((mine, dxs), (theirs, dxo))):
        for i in range(0, half, wide):
            cols = slice(h * half + i, h * half + i + wide)
            dots = lax.dot_general(held[:, cols], ts[...], TN, preferred_element_type=F32)
            buf[i : i + wide] = dots.astype(buf.dtype)
            send(buf.at[i : i + wide], out.at[i : i + wide])
    for j in range(0, pooled, step):
        part[j : j + step] = jnp.dot(held[j : j + step], x[...], preferred_element_type=F32).astype(BF)
        send(part.at[j : j + step], dy.at[j : j + step])
    for copy in copies:
        copy.wait()


def join_kernel(dxs, other, own, rest):
    own[...] = dxs[0:ROWS] + other[0:ROWS].astype(F32)
    rest[...] = (dxs[ROWS:] + other[ROWS:].astype(F32)).astype(BF)


def finish_kernel(scal, raw, *refs):
    total = refs[0][...].astype(F32)
    for part in refs[1:-1]:
        total += part[...].astype(F32)
    unit, norm = to_unit(raw[...])
    refs[-1][...] = from_unit(scal[0] * total, unit, norm)


def finish_texts_kernel(scal, raw, got, out):
    total = got[0].astype(F32)
    for k in range(1, got.shape[0]):
        total += got[k].astype(F32)
    unit, norm = to_unit(raw[...])
    out[...] = from_unit(scal[0] * total, unit, norm)


VMEM = pl.BlockSpec(memory_space=pltpu.VMEM)
SMEM = pl.BlockSpec(memory_space=pltpu.SMEM)
HBM = pl.BlockSpec(memory_space=pltpu.HBM)


def local(kernel, outs, args, smem=0, hbm=0, scratch=(), flops=0, nbytes=2**20, trans=0, vmem=8):
    specs = [SMEM] * smem + [HBM] * hbm
    return pl.pallas_call(
        kernel,
        out_shape=tuple((pltpu.HBM if spec is HBM else jax.ShapeDtypeStruct)(shape, dtype) for shape, dtype, spec in outs),
        in_specs=specs + [VMEM] * (len(args) - len(specs)),
        out_specs=tuple(spec for _, _, spec in outs),
        scratch_shapes=list(scratch),
        compiler_params=pltpu.CompilerParams(vmem_limit_bytes=vmem * 2**20),
        cost_estimate=pl.CostEstimate(flops=flops, bytes_accessed=nbytes, transcendentals=trans),
    )(*args)


def add(a, b):
    return (a.astype(F32) + b.astype(F32)).astype(BF)


def ring_gather(block):
    far = shifted(block, "z", 4)
    up = [block]
    down = [block]
    for _ in range(3):
        up.append(shifted(up[-1], "z", -1))
        down.append(shifted(down[-1], "z", 1))
    return up + [far] + down[:0:-1]


def near_reduce(rest):
    direct = [shifted(rest[k - 1], "z", k) for k in (4, 3, 5)]
    up, down = shifted(rest[1], "z", 1), shifted(rest[5], "z", -1)
    up, down = shifted(add(rest[0], up), "z", 1), shifted(add(rest[6], down), "z", -1)
    return direct + [up, down]


def on_device(images, texts, log_temp, bias):
    temp = jnp.exp(log_temp[0])
    rows, width = images.shape
    n_plane = lax.axis_size(PLANE)
    half = ROWS * lax.axis_size("z")
    pooled = ROWS * n_plane
    (spread,) = local(
        spread_kernel, [((n_plane, rows, width), BF, HBM)], [texts],
        scratch=[pltpu.VMEM((rows, width), BF), pltpu.SemaphoreType.DMA((n_plane,))],
    )
    spread, images = lax.optimization_barrier((spread, images))
    ts = swapped(spread, WHOLE).reshape(pooled, width)
    (x,) = local(unit_kernel, [((rows, width), BF, VMEM)], [images])
    (xs,) = local(pack_kernel, [((half, width), BF, VMEM)], ring_gather(x))
    xo = shifted(xs, "core", 1)
    at_x, at_y = lax.axis_index("x"), lax.axis_index(("yh", "yl"))
    place = jnp.where(lax.axis_index("core") == 0, 4 * at_y + at_x, 4 * at_x + at_y).astype(jnp.int32).reshape(1)
    scal = jnp.stack([temp, bias[0]])
    unit_flops = 2 * half * pooled * width
    dxs, dxo, dy = local(
        pair_kernel,
        [((half, width), F32, HBM), ((half, width), BF, HBM), ((pooled, width), BF, HBM)],
        [place, scal, xs, xo, ts], smem=2, hbm=2,
        scratch=[
            pltpu.VMEM((2 * half, width), BF),
            pltpu.VMEM((pooled, 2 * half), BF),
            pltpu.VMEM((half, width), F32),
            pltpu.VMEM((half, width), BF),
            pltpu.VMEM((pooled, width), BF),
            pltpu.SemaphoreType.DMA((8,)),
        ],
        flops=6 * unit_flops, nbytes=9 * 2**20, trans=4 * half * pooled, vmem=24,
    )
    half_way = swapped(dy.reshape(4, 4 * rows, width), OUTER)
    half_way = jnp.sum(half_way.astype(F32), axis=0).astype(BF)
    dyr = swapped(half_way.reshape(4, rows, width), INNER)
    other = shifted(dxo, "core", 1)
    own, rest = local(
        join_kernel, [((rows, width), F32, VMEM), ((half - rows, width), BF, VMEM)], [dxs, other],
        nbytes=5 * 2**20, vmem=16,
    )
    got = near_reduce(rest.reshape(-1, rows, width))
    (grad_images,) = local(finish_kernel, [((rows, width), F32, VMEM)], [scal, images, own] + got, smem=1)
    (grad_texts,) = local(finish_texts_kernel, [((rows, width), F32, VMEM)], [scal, texts, dyr], smem=1)
    return (grad_images, grad_texts)


def solution(mesh):
    fine = Mesh(mesh.devices.reshape(2, 4, 2, 2, 8), AXES)
    split = P(AXES, None)
    return jax.shard_map(
        on_device,
        mesh=fine,
        in_specs=(split, split, P(), P()),
        out_specs=(split, split),
        check_vma=False,
    )
```

```python
import jax
import jax.numpy as jnp
import numpy as np
from jax import lax
from jax.experimental import pallas as pl
from jax.experimental.pallas import tpu as pltpu
from jax.sharding import Mesh, PartitionSpec as P

AXES = ("yh", "x", "core", "yl", "z")
PLANE = ("yh", "x", "yl")
BF = jnp.bfloat16
F32 = jnp.float32
LOG2E = 1.4426950408889634
ROWS = 64
NT = (((1,), (1,)), ((), ()))
TN = (((0,), (0,)), ((), ()))


def plane_groups():
    at = np.arange(256).reshape(2, 4, 2, 2, 8)
    along_x, along_y = [], []
    for core in range(2):
        along_x.append(at[:, :, core].transpose(0, 2, 3, 1).reshape(-1, 4).tolist())
        along_y.append(at[:, :, core].transpose(1, 3, 0, 2).reshape(-1, 4).tolist())
    whole = at[:, :, 0].transpose(3, 0, 2, 1).reshape(-1, 16).tolist()
    whole += at[:, :, 1].transpose(3, 1, 0, 2).reshape(-1, 16).tolist()
    outer = along_y[0] + along_x[1]
    inner = along_x[0] + along_y[1]
    return whole, outer, inner


WHOLE, OUTER, INNER = plane_groups()


def swapped(blocks, groups):
    return lax.all_to_all(blocks, AXES, 0, 0, axis_index_groups=groups, tiled=True)


def shifted(block, axis, distance):
    n = lax.axis_size(axis)
    return lax.ppermute(block, axis, [(i, (i + distance) % n) for i in range(n)])


def to_unit(raw):
    norm = jnp.sqrt(jnp.sum(raw * raw, axis=1, keepdims=True) + 1e-06)
    return (raw / norm, norm)


def from_unit(grad, unit, norm):
    return (grad - unit * jnp.sum(unit * grad, axis=1, keepdims=True)) / norm


def unit_rows(raw):
    norm = jnp.sqrt(jnp.sum(raw * raw, axis=1, keepdims=True) + 1e-06)
    return (raw / norm).astype(BF)


def spread_kernel(raw, out, unit, sems):
    unit[...] = unit_rows(raw[...])
    copies = [pltpu.make_async_copy(unit, out.at[k], sems.at[k]) for k in range(out.shape[0])]
    for copy in copies:
        copy.start()
    for copy in copies:
        copy.wait()


def unit_kernel(raw, out):
    out[...] = unit_rows(raw[...])


def pack_kernel(*refs):
    for k, block in enumerate(refs[:-1]):
        refs[-1][k * ROWS : (k + 1) * ROWS] = block[...]


def sigmoid(temp, offset, dots):
    return 1.0 / (1.0 + jnp.exp2(dots * (temp * -LOG2E) + offset * -LOG2E))


def pair_kernel(place, scal, xs, xo, ts, dxs, dxo, dy, x, held, mine, theirs, part, sems):
    temp = scal[0]
    offset = scal[1]
    half = xs.shape[0]
    pooled = ts.shape[0]
    wide = 512
    step = 256
    loads = [
        pltpu.make_async_copy(xs, x.at[0:half], sems.at[0]),
        pltpu.make_async_copy(xo, x.at[half : 2 * half], sems.at[1]),
    ]
    for copy in loads:
        copy.start()
    for h, copy in enumerate(loads):
        copy.wait()
        cols = slice(h * half, (h + 1) * half)
        for j in range(pooled // step):
            sl = pl.ds(j * step, step)
            dots = lax.dot_general(ts[sl], x[cols], NT, preferred_element_type=F32)
            held[sl, cols] = sigmoid(temp, offset, dots).astype(BF)
    at = pl.multiple_of(place[0] * ROWS, ROWS)
    dots = lax.dot_general(ts[pl.ds(at, ROWS)], x[0:ROWS], NT, preferred_element_type=F32)
    eye = lax.broadcasted_iota(jnp.int32, (ROWS, ROWS), 0) == lax.broadcasted_iota(
        jnp.int32, (ROWS, ROWS), 1
    )
    held[pl.ds(at, ROWS), 0:ROWS] = (sigmoid(temp, offset, dots) - eye.astype(F32)).astype(BF)
    copies = []

    def send(src, dst):
        copies.append(pltpu.make_async_copy(src, dst, sems.at[2 + len(copies)]))
        copies[-1].start()

    for h, (buf, out) in enumerate(((mine, dxs), (theirs, dxo))):
        for i in range(0, half, wide):
            cols = slice(h * half + i, h * half + i + wide)
            dots = lax.dot_general(held[:, cols], ts[...], TN, preferred_element_type=F32)
            buf[i : i + wide] = dots.astype(buf.dtype)
            send(buf.at[i : i + wide], out.at[i : i + wide])
    for j in range(0, pooled, step):
        part[j : j + step] = jnp.dot(held[j : j + step], x[...], preferred_element_type=F32).astype(BF)
        send(part.at[j : j + step], dy.at[j : j + step])
    for copy in copies:
        copy.wait()


def join_kernel(dxs, other, own, rest):
    own[...] = dxs[0:ROWS] + other[0:ROWS].astype(F32)
    rest[...] = (dxs[ROWS:] + other[ROWS:].astype(F32)).astype(BF)


def finish_kernel(scal, raw, *refs):
    total = refs[0][...].astype(F32)
    for part in refs[1:-1]:
        total += part[...].astype(F32)
    unit, norm = to_unit(raw[...])
    refs[-1][...] = from_unit(scal[0] * total, unit, norm)


def sum_kernel(got, out, part, sems):
    copies = []
    for j in range(out.shape[0]):
        total = got[0, j].astype(F32)
        for k in range(1, got.shape[0]):
            total += got[k, j].astype(F32)
        part[j] = total.astype(BF)
        copies.append(pltpu.make_async_copy(part.at[j], out.at[j], sems.at[j]))
        copies[-1].start()
    for copy in copies:
        copy.wait()


def finish_texts_kernel(scal, raw, got, out):
    total = got[0].astype(F32)
    for k in range(1, got.shape[0]):
        total += got[k].astype(F32)
    unit, norm = to_unit(raw[...])
    out[...] = from_unit(scal[0] * total, unit, norm)


VMEM = pl.BlockSpec(memory_space=pltpu.VMEM)
SMEM = pl.BlockSpec(memory_space=pltpu.SMEM)
HBM = pl.BlockSpec(memory_space=pltpu.HBM)


def local(kernel, outs, args, smem=0, hbm=0, scratch=(), flops=0, nbytes=2**20, trans=0, vmem=8):
    specs = [SMEM] * smem + [HBM] * hbm
    return pl.pallas_call(
        kernel,
        out_shape=tuple((pltpu.HBM if spec is HBM else jax.ShapeDtypeStruct)(shape, dtype) for shape, dtype, spec in outs),
        in_specs=specs + [VMEM] * (len(args) - len(specs)),
        out_specs=tuple(spec for _, _, spec in outs),
        scratch_shapes=list(scratch),
        compiler_params=pltpu.CompilerParams(vmem_limit_bytes=vmem * 2**20),
        cost_estimate=pl.CostEstimate(flops=flops, bytes_accessed=nbytes, transcendentals=trans),
    )(*args)


def add(a, b):
    return (a.astype(F32) + b.astype(F32)).astype(BF)


def ring_gather(block, scalars):
    far = shifted(block, "z", 4)
    up = [block]
    down = [block]
    for k in range(3):
        up.append(shifted(up[-1], "z", -1))
        down.append(shifted(down[-1], "z", 1))
        if k == 0:
            up[-1], scalars = lax.optimization_barrier((up[-1], scalars))
    return up + [far] + down[:0:-1], scalars


def direct_reduce(rest):
    return [shifted(rest[k - 1], "z", k) for k in (4, 3, 5, 2, 6, 1, 7)]


def on_device(images, texts, log_temp, bias):
    temp = jnp.exp(log_temp[0])
    rows, width = images.shape
    n_plane = lax.axis_size(PLANE)
    half = ROWS * lax.axis_size("z")
    pooled = ROWS * n_plane
    (spread,) = local(
        spread_kernel, [((n_plane, rows, width), BF, HBM)], [texts],
        scratch=[pltpu.VMEM((rows, width), BF), pltpu.SemaphoreType.DMA((n_plane,))],
    )
    spread, images = lax.optimization_barrier((spread, images))
    ts = swapped(spread, WHOLE).reshape(pooled, width)
    (x,) = local(unit_kernel, [((rows, width), BF, VMEM)], [images])
    at_x, at_y = lax.axis_index("x"), lax.axis_index(("yh", "yl"))
    place = jnp.where(lax.axis_index("core") == 0, 4 * at_y + at_x, 4 * at_x + at_y).astype(jnp.int32).reshape(1)
    scal = jnp.stack([temp, bias[0]])
    blocks, (place, scal) = ring_gather(x, (place, scal))
    (xs,) = local(pack_kernel, [((half, width), BF, VMEM)], blocks)
    xo = shifted(xs, "core", 1)
    unit_flops = 2 * half * pooled * width
    dxs, dxo, dy = local(
        pair_kernel,
        [((half, width), F32, HBM), ((half, width), BF, HBM), ((pooled, width), BF, HBM)],
        [place, scal, xs, xo, ts], smem=2, hbm=2,
        scratch=[
            pltpu.VMEM((2 * half, width), BF),
            pltpu.VMEM((pooled, 2 * half), BF),
            pltpu.VMEM((half, width), F32),
            pltpu.VMEM((half, width), BF),
            pltpu.VMEM((pooled, width), BF),
            pltpu.SemaphoreType.DMA((8,)),
        ],
        flops=6 * unit_flops, nbytes=9 * 2**20, trans=4 * half * pooled, vmem=24,
    )
    half_way = swapped(dy.reshape(4, 4 * rows, width), OUTER)
    (half_way,) = local(
        sum_kernel, [((4, rows, width), BF, HBM)], [half_way.reshape(4, 4, rows, width)], nbytes=3 * 2**20, vmem=16,
        scratch=[pltpu.VMEM((4, rows, width), BF), pltpu.SemaphoreType.DMA((4,))],
    )
    dyr = swapped(half_way, INNER)
    other = shifted(dxo, "core", 1)
    own, rest = local(
        join_kernel, [((rows, width), F32, VMEM), ((half - rows, width), BF, VMEM)], [dxs, other],
        nbytes=5 * 2**20, vmem=16,
    )
    got = direct_reduce(rest.reshape(-1, rows, width))
    (grad_images,) = local(finish_kernel, [((rows, width), F32, VMEM)], [scal, images, own] + got, smem=1)
    (grad_texts,) = local(finish_texts_kernel, [((rows, width), F32, VMEM)], [scal, texts, dyr], smem=1)
    return (grad_images, grad_texts)


def solution(mesh):
    fine = Mesh(mesh.devices.reshape(2, 4, 2, 2, 8), AXES)
    split = P(AXES, None)
    return jax.shard_map(
        on_device,
        mesh=fine,
        in_specs=(split, split, P(), P()),
        out_specs=(split, split),
        check_vma=False,
    )
```

```python
import jax
import jax.numpy as jnp
import numpy as np
from jax import lax
from jax.experimental import pallas as pl
from jax.experimental.pallas import tpu as pltpu
from jax.sharding import Mesh, PartitionSpec as P

AXES = ("yh", "x", "core", "yl", "z")
PLANE = ("yh", "x", "yl")
BF = jnp.bfloat16
F32 = jnp.float32
LOG2E = 1.4426950408889634
ROWS = 64
NT = (((1,), (1,)), ((), ()))
TN = (((0,), (0,)), ((), ()))


def plane_groups():
    at = np.arange(256).reshape(2, 4, 2, 2, 8)
    along_x, along_y = [], []
    for core in range(2):
        along_x.append(at[:, :, core].transpose(0, 2, 3, 1).reshape(-1, 4).tolist())
        along_y.append(at[:, :, core].transpose(1, 3, 0, 2).reshape(-1, 4).tolist())
    whole = at[:, :, 0].transpose(3, 0, 2, 1).reshape(-1, 16).tolist()
    whole += at[:, :, 1].transpose(3, 1, 0, 2).reshape(-1, 16).tolist()
    outer = along_y[0] + along_x[1]
    inner = along_x[0] + along_y[1]
    return whole, outer, inner


WHOLE, OUTER, INNER = plane_groups()


def swapped(blocks, groups):
    return lax.all_to_all(blocks, AXES, 0, 0, axis_index_groups=groups, tiled=True)


def shifted(block, axis, distance):
    n = lax.axis_size(axis)
    return lax.ppermute(block, axis, [(i, (i + distance) % n) for i in range(n)])


def to_unit(raw):
    norm = jnp.sqrt(jnp.sum(raw * raw, axis=1, keepdims=True) + 1e-06)
    return (raw / norm, norm)


def from_unit(grad, unit, norm):
    return (grad - unit * jnp.sum(unit * grad, axis=1, keepdims=True)) / norm


def unit_rows(raw):
    norm = jnp.sqrt(jnp.sum(raw * raw, axis=1, keepdims=True) + 1e-06)
    return (raw / norm).astype(BF)


def spread_kernel(raw, out, unit, sems):
    unit[...] = unit_rows(raw[...])
    copies = [pltpu.make_async_copy(unit, out.at[k], sems.at[k]) for k in range(out.shape[0])]
    for copy in copies:
        copy.start()
    for copy in copies:
        copy.wait()


def unit_kernel(raw, out):
    out[...] = unit_rows(raw[...])


def pack_kernel(*refs):
    for k, block in enumerate(refs[:-1]):
        refs[-1][k * ROWS : (k + 1) * ROWS] = block[...]


def sigmoid(temp, offset, dots):
    return 1.0 / (1.0 + jnp.exp2(dots * (temp * -LOG2E) + offset * -LOG2E))


def pair_kernel(place, scal, xs, xo, ts, dxs, dxo, dy, x, held, mine, theirs, part, sems):
    temp = scal[0]
    offset = scal[1]
    half = xs.shape[0]
    pooled = ts.shape[0]
    wide = 512
    step = 256
    loads = [
        pltpu.make_async_copy(xs, x.at[0:half], sems.at[0]),
        pltpu.make_async_copy(xo, x.at[half : 2 * half], sems.at[1]),
    ]
    for copy in loads:
        copy.start()
    for h, copy in enumerate(loads):
        copy.wait()
        cols = slice(h * half, (h + 1) * half)
        for j in range(pooled // step):
            sl = pl.ds(j * step, step)
            dots = lax.dot_general(ts[sl], x[cols], NT, preferred_element_type=F32)
            held[sl, cols] = sigmoid(temp, offset, dots).astype(BF)
    at = pl.multiple_of(place[0] * ROWS, ROWS)
    dots = lax.dot_general(ts[pl.ds(at, ROWS)], x[0:ROWS], NT, preferred_element_type=F32)
    eye = lax.broadcasted_iota(jnp.int32, (ROWS, ROWS), 0) == lax.broadcasted_iota(
        jnp.int32, (ROWS, ROWS), 1
    )
    held[pl.ds(at, ROWS), 0:ROWS] = (sigmoid(temp, offset, dots) - eye.astype(F32)).astype(BF)
    copies = []

    def send(src, dst):
        copies.append(pltpu.make_async_copy(src, dst, sems.at[2 + len(copies)]))
        copies[-1].start()

    for h, (buf, out) in enumerate(((mine, dxs), (theirs, dxo))):
        for i in range(0, half, wide):
            cols = slice(h * half + i, h * half + i + wide)
            dots = lax.dot_general(held[:, cols], ts[...], TN, preferred_element_type=F32)
            buf[i : i + wide] = dots.astype(buf.dtype)
            send(buf.at[i : i + wide], out.at[i : i + wide])
    for j in range(0, pooled, step):
        part[j : j + step] = jnp.dot(held[j : j + step], x[...], preferred_element_type=F32).astype(BF)
        send(part.at[j : j + step], dy.at[j : j + step])
    for copy in copies:
        copy.wait()


def join_kernel(dxs, other, own, rest):
    own[...] = dxs[0:ROWS] + other[0:ROWS].astype(F32)
    rest[...] = (dxs[ROWS:] + other[ROWS:].astype(F32)).astype(BF)


def finish_kernel(scal, raw, *refs):
    total = refs[0][...].astype(F32)
    for part in refs[1:-1]:
        total += part[...].astype(F32)
    unit, norm = to_unit(raw[...])
    refs[-1][...] = from_unit(scal[0] * total, unit, norm)


def sum_kernel(got, out, part, sems):
    copies = []
    for j in range(out.shape[0]):
        total = got[0, j].astype(F32)
        for k in range(1, got.shape[0]):
            total += got[k, j].astype(F32)
        part[j] = total.astype(BF)
        copies.append(pltpu.make_async_copy(part.at[j], out.at[j], sems.at[j]))
        copies[-1].start()
    for copy in copies:
        copy.wait()


def finish_texts_kernel(scal, raw, got, out):
    total = got[0].astype(F32)
    for k in range(1, got.shape[0]):
        total += got[k].astype(F32)
    unit, norm = to_unit(raw[...])
    out[...] = from_unit(scal[0] * total, unit, norm)


VMEM = pl.BlockSpec(memory_space=pltpu.VMEM)
SMEM = pl.BlockSpec(memory_space=pltpu.SMEM)
HBM = pl.BlockSpec(memory_space=pltpu.HBM)


def local(kernel, outs, args, smem=0, hbm=0, scratch=(), flops=0, nbytes=2**20, trans=0, vmem=8):
    specs = [SMEM] * smem + [HBM] * hbm
    return pl.pallas_call(
        kernel,
        out_shape=tuple((pltpu.HBM if spec is HBM else jax.ShapeDtypeStruct)(shape, dtype) for shape, dtype, spec in outs),
        in_specs=specs + [VMEM] * (len(args) - len(specs)),
        out_specs=tuple(spec for _, _, spec in outs),
        scratch_shapes=list(scratch),
        compiler_params=pltpu.CompilerParams(vmem_limit_bytes=vmem * 2**20),
        cost_estimate=pl.CostEstimate(flops=flops, bytes_accessed=nbytes, transcendentals=trans),
    )(*args)


def add(a, b):
    return (a.astype(F32) + b.astype(F32)).astype(BF)


def ring_gather(block):
    far = shifted(block, "z", 4)
    up = [block]
    down = [block]
    for _ in range(3):
        up.append(shifted(up[-1], "z", -1))
        down.append(shifted(down[-1], "z", 1))
    return up + [far] + down[:0:-1]


def near_reduce(rest):
    direct = [shifted(rest[k - 1], "z", k) for k in (4, 3, 5)]
    up, down = shifted(rest[1], "z", 1), shifted(rest[5], "z", -1)
    up, down = shifted(add(rest[0], up), "z", 1), shifted(add(rest[6], down), "z", -1)
    return direct + [up, down]


def on_device(images, texts, log_temp, bias):
    temp = jnp.exp(log_temp[0])
    rows, width = images.shape
    n_plane = lax.axis_size(PLANE)
    half = ROWS * lax.axis_size("z")
    pooled = ROWS * n_plane
    (spread,) = local(
        spread_kernel, [((n_plane, rows, width), BF, HBM)], [texts],
        scratch=[pltpu.VMEM((rows, width), BF), pltpu.SemaphoreType.DMA((n_plane,))],
    )
    spread, images = lax.optimization_barrier((spread, images))
    ts = swapped(spread, WHOLE).reshape(pooled, width)
    (x,) = local(unit_kernel, [((rows, width), BF, VMEM)], [images])
    (xs,) = local(pack_kernel, [((half, width), BF, VMEM)], ring_gather(x))
    xo = shifted(xs, "core", 1)
    at_x, at_y = lax.axis_index("x"), lax.axis_index(("yh", "yl"))
    place = jnp.where(lax.axis_index("core") == 0, 4 * at_y + at_x, 4 * at_x + at_y).astype(jnp.int32).reshape(1)
    scal = jnp.stack([temp, bias[0]])
    unit_flops = 2 * half * pooled * width
    dxs, dxo, dy = local(
        pair_kernel,
        [((half, width), F32, HBM), ((half, width), BF, HBM), ((pooled, width), BF, HBM)],
        [place, scal, xs, xo, ts], smem=2, hbm=2,
        scratch=[
            pltpu.VMEM((2 * half, width), BF),
            pltpu.VMEM((pooled, 2 * half), BF),
            pltpu.VMEM((half, width), F32),
            pltpu.VMEM((half, width), BF),
            pltpu.VMEM((pooled, width), BF),
            pltpu.SemaphoreType.DMA((8,)),
        ],
        flops=6 * unit_flops, nbytes=9 * 2**20, trans=4 * half * pooled, vmem=24,
    )
    half_way = swapped(dy.reshape(4, 4 * rows, width), OUTER)
    other = shifted(dxo, "core", 1)
    own, rest = local(
        join_kernel, [((rows, width), F32, VMEM), ((half - rows, width), BF, VMEM)], [dxs, other],
        nbytes=5 * 2**20, vmem=16,
    )
    got = near_reduce(rest.reshape(-1, rows, width))
    half_way, *got[3:] = lax.optimization_barrier((half_way, *got[3:]))
    (half_way,) = local(
        sum_kernel, [((4, rows, width), BF, HBM)], [half_way.reshape(4, 4, rows, width)], nbytes=3 * 2**20, vmem=16,
        scratch=[pltpu.VMEM((4, rows, width), BF), pltpu.SemaphoreType.DMA((4,))],
    )
    dyr = swapped(half_way, INNER)
    (grad_images,) = local(finish_kernel, [((rows, width), F32, VMEM)], [scal, images, own] + got, smem=1)
    (grad_texts,) = local(finish_texts_kernel, [((rows, width), F32, VMEM)], [scal, texts, dyr], smem=1)
    return (grad_images, grad_texts)


def solution(mesh):
    fine = Mesh(mesh.devices.reshape(2, 4, 2, 2, 8), AXES)
    split = P(AXES, None)
    return jax.shard_map(
        on_device,
        mesh=fine,
        in_specs=(split, split, P(), P()),
        out_specs=(split, split),
        check_vma=False,
    )
```

```python
import jax
import jax.numpy as jnp
import numpy as np
from jax import lax
from jax.experimental import pallas as pl
from jax.experimental.pallas import tpu as pltpu
from jax.sharding import Mesh, PartitionSpec as P

AXES = ("yh", "x", "core", "yl", "z")
PLANE = ("yh", "x", "yl")
BF = jnp.bfloat16
F32 = jnp.float32
LOG2E = 1.4426950408889634
ROWS = 64
NT = (((1,), (1,)), ((), ()))
TN = (((0,), (0,)), ((), ()))


def plane_groups():
    at = np.arange(256).reshape(2, 4, 2, 2, 8)
    along_x, along_y = [], []
    for core in range(2):
        along_x.append(at[:, :, core].transpose(0, 2, 3, 1).reshape(-1, 4).tolist())
        along_y.append(at[:, :, core].transpose(1, 3, 0, 2).reshape(-1, 4).tolist())
    whole = at[:, :, 0].transpose(3, 0, 2, 1).reshape(-1, 16).tolist()
    whole += at[:, :, 1].transpose(3, 1, 0, 2).reshape(-1, 16).tolist()
    outer = along_y[0] + along_x[1]
    inner = along_x[0] + along_y[1]
    return whole, outer, inner


WHOLE, OUTER, INNER = plane_groups()


def swapped(blocks, groups):
    return lax.all_to_all(blocks, AXES, 0, 0, axis_index_groups=groups, tiled=True)


def shifted(block, axis, distance):
    n = lax.axis_size(axis)
    return lax.ppermute(block, axis, [(i, (i + distance) % n) for i in range(n)])


def to_unit(raw):
    norm = jnp.sqrt(jnp.sum(raw * raw, axis=1, keepdims=True) + 1e-06)
    return (raw / norm, norm)


def from_unit(grad, unit, norm):
    return (grad - unit * jnp.sum(unit * grad, axis=1, keepdims=True)) / norm


def unit_rows(raw):
    norm = jnp.sqrt(jnp.sum(raw * raw, axis=1, keepdims=True) + 1e-06)
    return (raw / norm).astype(BF)


def spread_kernel(raw, out, unit, sems):
    unit[...] = unit_rows(raw[...])
    copies = [pltpu.make_async_copy(unit, out.at[k], sems.at[k]) for k in range(out.shape[0])]
    for copy in copies:
        copy.start()
    for copy in copies:
        copy.wait()


def unit_kernel(raw, out):
    out[...] = unit_rows(raw[...])


def pack_kernel(*refs):
    for k, block in enumerate(refs[:-1]):
        refs[-1][k * ROWS : (k + 1) * ROWS] = block[...]


def sigmoid(temp, offset, dots):
    return 1.0 / (1.0 + jnp.exp2(dots * (temp * -LOG2E) + offset * -LOG2E))


def pair_kernel(place, scal, xs, xo, ts, dxs, dxo, dy, x, held, mine, theirs, part, sems):
    temp = scal[0]
    offset = scal[1]
    half = xs.shape[0]
    pooled = ts.shape[0]
    wide = 512
    step = 256
    loads = [
        pltpu.make_async_copy(xs, x.at[0:half], sems.at[0]),
        pltpu.make_async_copy(xo, x.at[half : 2 * half], sems.at[1]),
    ]
    for copy in loads:
        copy.start()
    for h, copy in enumerate(loads):
        copy.wait()
        cols = slice(h * half, (h + 1) * half)
        for j in range(pooled // step):
            sl = pl.ds(j * step, step)
            dots = lax.dot_general(ts[sl], x[cols], NT, preferred_element_type=F32)
            held[sl, cols] = sigmoid(temp, offset, dots).astype(BF)
    at = pl.multiple_of(place[0] * ROWS, ROWS)
    dots = lax.dot_general(ts[pl.ds(at, ROWS)], x[0:ROWS], NT, preferred_element_type=F32)
    eye = lax.broadcasted_iota(jnp.int32, (ROWS, ROWS), 0) == lax.broadcasted_iota(
        jnp.int32, (ROWS, ROWS), 1
    )
    held[pl.ds(at, ROWS), 0:ROWS] = (sigmoid(temp, offset, dots) - eye.astype(F32)).astype(BF)
    copies = []

    def send(src, dst):
        copies.append(pltpu.make_async_copy(src, dst, sems.at[2 + len(copies)]))
        copies[-1].start()

    for h, (buf, out) in enumerate(((mine, dxs), (theirs, dxo))):
        for i in range(0, half, wide):
            cols = slice(h * half + i, h * half + i + wide)
            dots = lax.dot_general(held[:, cols], ts[...], TN, preferred_element_type=F32)
            buf[i : i + wide] = dots.astype(buf.dtype)
            send(buf.at[i : i + wide], out.at[i : i + wide])
    for j in range(0, pooled, step):
        part[j : j + step] = jnp.dot(held[j : j + step], x[...], preferred_element_type=F32).astype(BF)
        send(part.at[j : j + step], dy.at[j : j + step])
    for copy in copies:
        copy.wait()


def join_kernel(dxs, other, *outs):
    for k, out in enumerate(outs):
        sl = slice(k * ROWS, (k + 1) * ROWS)
        out[...] = (dxs[sl] + other[sl].astype(F32)).astype(out.dtype)


def finish_kernel(scal, raw, *refs):
    total = refs[0][...].astype(F32)
    for part in refs[1:-1]:
        total += part[...].astype(F32)
    unit, norm = to_unit(raw[...])
    refs[-1][...] = from_unit(scal[0] * total, unit, norm)


def sum_kernel(got, out, part, sems):
    copies = []
    for j in range(out.shape[0]):
        total = got[0, j].astype(F32)
        for k in range(1, got.shape[0]):
            total += got[k, j].astype(F32)
        part[j] = total.astype(BF)
        copies.append(pltpu.make_async_copy(part.at[j], out.at[j], sems.at[j]))
        copies[-1].start()
    for copy in copies:
        copy.wait()


def finish_texts_kernel(scal, raw, got, out):
    total = got[0].astype(F32)
    for k in range(1, got.shape[0]):
        total += got[k].astype(F32)
    unit, norm = to_unit(raw[...])
    out[...] = from_unit(scal[0] * total, unit, norm)


VMEM = pl.BlockSpec(memory_space=pltpu.VMEM)
SMEM = pl.BlockSpec(memory_space=pltpu.SMEM)
HBM = pl.BlockSpec(memory_space=pltpu.HBM)


def local(kernel, outs, args, smem=0, hbm=0, scratch=(), flops=0, nbytes=2**20, trans=0, vmem=8):
    specs = [SMEM] * smem + [HBM] * hbm
    return pl.pallas_call(
        kernel,
        out_shape=tuple((pltpu.HBM if spec is HBM else jax.ShapeDtypeStruct)(shape, dtype) for shape, dtype, spec in outs),
        in_specs=specs + [VMEM] * (len(args) - len(specs)),
        out_specs=tuple(spec for _, _, spec in outs),
        scratch_shapes=list(scratch),
        compiler_params=pltpu.CompilerParams(vmem_limit_bytes=vmem * 2**20),
        cost_estimate=pl.CostEstimate(flops=flops, bytes_accessed=nbytes, transcendentals=trans),
    )(*args)


def add(a, b):
    return (a.astype(F32) + b.astype(F32)).astype(BF)


def ring_gather(block):
    far = shifted(block, "z", 4)
    up = [block]
    down = [block]
    for _ in range(3):
        up.append(shifted(up[-1], "z", -1))
        down.append(shifted(down[-1], "z", 1))
    return up + [far] + down[:0:-1]


def ring_step(up, down):
    return shifted(up, "z", 1), shifted(down, "z", -1)


def on_device(images, texts, log_temp, bias):
    temp = jnp.exp(log_temp[0])
    rows, width = images.shape
    n_plane = lax.axis_size(PLANE)
    half = ROWS * lax.axis_size("z")
    pooled = ROWS * n_plane
    (spread,) = local(
        spread_kernel, [((n_plane, rows, width), BF, HBM)], [texts],
        scratch=[pltpu.VMEM((rows, width), BF), pltpu.SemaphoreType.DMA((n_plane,))],
    )
    spread, images = lax.optimization_barrier((spread, images))
    ts = swapped(spread, WHOLE).reshape(pooled, width)
    (x,) = local(unit_kernel, [((rows, width), BF, VMEM)], [images])
    (xs,) = local(pack_kernel, [((half, width), BF, VMEM)], ring_gather(x))
    xo = shifted(xs, "core", 1)
    at_x, at_y = lax.axis_index("x"), lax.axis_index(("yh", "yl"))
    place = jnp.where(lax.axis_index("core") == 0, 4 * at_y + at_x, 4 * at_x + at_y).astype(jnp.int32).reshape(1)
    scal = jnp.stack([temp, bias[0]])
    unit_flops = 2 * half * pooled * width
    dxs, dxo, dy = local(
        pair_kernel,
        [((half, width), F32, HBM), ((half, width), BF, HBM), ((pooled, width), BF, HBM)],
        [place, scal, xs, xo, ts], smem=2, hbm=2,
        scratch=[
            pltpu.VMEM((2 * half, width), BF),
            pltpu.VMEM((pooled, 2 * half), BF),
            pltpu.VMEM((half, width), F32),
            pltpu.VMEM((half, width), BF),
            pltpu.VMEM((pooled, width), BF),
            pltpu.SemaphoreType.DMA((8,)),
        ],
        flops=6 * unit_flops, nbytes=9 * 2**20, trans=4 * half * pooled, vmem=24,
    )
    half_way = swapped(dy.reshape(4, 4 * rows, width), OUTER)
    other = shifted(dxo, "core", 1)
    parts = local(
        join_kernel, [((rows, width), BF if k else F32, VMEM) for k in range(half // rows)], [dxs, other],
        nbytes=5 * 2**20, vmem=16,
    )
    far = shifted(parts[4], "z", 4)
    up, down = ring_step(parts[3], parts[5])
    up, down = ring_step(add(parts[2], up), add(parts[6], down))
    up, down = add(parts[1], up), add(parts[7], down)
    half_way, far, up, down = lax.optimization_barrier((half_way, far, up, down))
    (half_way,) = local(
        sum_kernel, [((4, rows, width), BF, HBM)], [half_way.reshape(4, 4, rows, width)], nbytes=3 * 2**20, vmem=16,
        scratch=[pltpu.VMEM((4, rows, width), BF), pltpu.SemaphoreType.DMA((4,))],
    )
    up, down = ring_step(up, down)
    dyr = swapped(half_way, INNER)
    (grad_images,) = local(finish_kernel, [((rows, width), F32, VMEM)], [scal, images, parts[0], far, up, down], smem=1)
    (grad_texts,) = local(finish_texts_kernel, [((rows, width), F32, VMEM)], [scal, texts, dyr], smem=1)
    return (grad_images, grad_texts)


def solution(mesh):
    fine = Mesh(mesh.devices.reshape(2, 4, 2, 2, 8), AXES)
    split = P(AXES, None)
    return jax.shard_map(
        on_device,
        mesh=fine,
        in_specs=(split, split, P(), P()),
        out_specs=(split, split),
        check_vma=False,
    )
```

```python
import jax
import jax.numpy as jnp
import numpy as np
from jax import lax
from jax.experimental import pallas as pl
from jax.experimental.pallas import tpu as pltpu
from jax.sharding import Mesh, PartitionSpec as P

AXES = ("yh", "x", "core", "yl", "z")
PLANE = ("yh", "x", "yl")
BF = jnp.bfloat16
F32 = jnp.float32
LOG2E = 1.4426950408889634
ROWS = 64
NT = (((1,), (1,)), ((), ()))
TN = (((0,), (0,)), ((), ()))


def plane_groups():
    at = np.arange(256).reshape(2, 4, 2, 2, 8)
    along_x, along_y = [], []
    for core in range(2):
        along_x.append(at[:, :, core].transpose(0, 2, 3, 1).reshape(-1, 4).tolist())
        along_y.append(at[:, :, core].transpose(1, 3, 0, 2).reshape(-1, 4).tolist())
    whole = at[:, :, 0].transpose(3, 0, 2, 1).reshape(-1, 16).tolist()
    whole += at[:, :, 1].transpose(3, 1, 0, 2).reshape(-1, 16).tolist()
    outer = along_y[0] + along_x[1]
    inner = along_x[0] + along_y[1]
    return whole, outer, inner


WHOLE, OUTER, INNER = plane_groups()


def swapped(blocks, groups):
    return lax.all_to_all(blocks, AXES, 0, 0, axis_index_groups=groups, tiled=True)


def shifted(block, axis, distance):
    n = lax.axis_size(axis)
    return lax.ppermute(block, axis, [(i, (i + distance) % n) for i in range(n)])


def to_unit(raw):
    norm = jnp.sqrt(jnp.sum(raw * raw, axis=1, keepdims=True) + 1e-06)
    return (raw / norm, norm)


def from_unit(grad, unit, norm):
    return (grad - unit * jnp.sum(unit * grad, axis=1, keepdims=True)) / norm


def unit_rows(raw):
    norm = jnp.sqrt(jnp.sum(raw * raw, axis=1, keepdims=True) + 1e-06)
    return (raw / norm).astype(BF)


def spread_kernel(raw, out, unit, sems):
    unit[...] = unit_rows(raw[...])
    copies = [pltpu.make_async_copy(unit, out.at[k], sems.at[k]) for k in range(out.shape[0])]
    for copy in copies:
        copy.start()
    for copy in copies:
        copy.wait()


def unit_kernel(raw, out):
    out[...] = unit_rows(raw[...])


def pack_kernel(*refs):
    for k, block in enumerate(refs[:-1]):
        refs[-1][k * ROWS : (k + 1) * ROWS] = block[...]


def sigmoid(temp, offset, dots):
    return 1.0 / (1.0 + jnp.exp2(dots * (temp * -LOG2E) + offset * -LOG2E))


def pair_kernel(place, scal, xs, xo, ts, dxs, dxo, dy, x, held, mine, theirs, part, sems):
    temp = scal[0]
    offset = scal[1]
    half = xs.shape[0]
    pooled = ts.shape[0]
    wide = 512
    step = 256
    loads = [
        pltpu.make_async_copy(xs, x.at[0:half], sems.at[0]),
        pltpu.make_async_copy(xo, x.at[half : 2 * half], sems.at[1]),
    ]
    for copy in loads:
        copy.start()
    for h, copy in enumerate(loads):
        copy.wait()
        cols = slice(h * half, (h + 1) * half)
        for j in range(pooled // step):
            sl = pl.ds(j * step, step)
            dots = lax.dot_general(ts[sl], x[cols], NT, preferred_element_type=F32)
            held[sl, cols] = sigmoid(temp, offset, dots).astype(BF)
    at = pl.multiple_of(place[0] * ROWS, ROWS)
    dots = lax.dot_general(ts[pl.ds(at, ROWS)], x[0:ROWS], NT, preferred_element_type=F32)
    eye = lax.broadcasted_iota(jnp.int32, (ROWS, ROWS), 0) == lax.broadcasted_iota(
        jnp.int32, (ROWS, ROWS), 1
    )
    held[pl.ds(at, ROWS), 0:ROWS] = (sigmoid(temp, offset, dots) - eye.astype(F32)).astype(BF)
    copies = []

    def send(src, dst):
        copies.append(pltpu.make_async_copy(src, dst, sems.at[2 + len(copies)]))
        copies[-1].start()

    for h, (buf, out) in enumerate(((mine, dxs), (theirs, dxo))):
        for i in range(0, half, wide):
            cols = slice(h * half + i, h * half + i + wide)
            dots = lax.dot_general(held[:, cols], ts[...], TN, preferred_element_type=F32)
            buf[i : i + wide] = dots.astype(buf.dtype)
            send(buf.at[i : i + wide], out.at[i : i + wide])
    for j in range(0, pooled, step):
        part[j : j + step] = jnp.dot(held[j : j + step], x[...], preferred_element_type=F32).astype(BF)
        send(part.at[j : j + step], dy.at[j : j + step])
    for copy in copies:
        copy.wait()


def join_kernel(dxs, other, own, rest):
    own[...] = dxs[0:ROWS] + other[0:ROWS].astype(F32)
    rest[...] = (dxs[ROWS:] + other[ROWS:].astype(F32)).astype(BF)


def finish_kernel(scal, raw, *refs):
    total = refs[0][...].astype(F32)
    for part in refs[1:-1]:
        total += part[...].astype(F32)
    unit, norm = to_unit(raw[...])
    refs[-1][...] = from_unit(scal[0] * total, unit, norm)


def sum_kernel(got, out, part, sems):
    copies = []
    for j in range(out.shape[0]):
        total = got[0, j].astype(F32)
        for k in range(1, got.shape[0]):
            total += got[k, j].astype(F32)
        part[j] = total.astype(BF)
        copies.append(pltpu.make_async_copy(part.at[j], out.at[j], sems.at[j]))
        copies[-1].start()
    for copy in copies:
        copy.wait()


def finish_texts_kernel(scal, raw, got, out):
    total = got[0].astype(F32)
    for k in range(1, got.shape[0]):
        total += got[k].astype(F32)
    unit, norm = to_unit(raw[...])
    out[...] = from_unit(scal[0] * total, unit, norm)


VMEM = pl.BlockSpec(memory_space=pltpu.VMEM)
SMEM = pl.BlockSpec(memory_space=pltpu.SMEM)
HBM = pl.BlockSpec(memory_space=pltpu.HBM)


def local(kernel, outs, args, smem=0, hbm=0, scratch=(), flops=0, nbytes=2**20, trans=0, vmem=8):
    specs = [SMEM] * smem + [HBM] * hbm
    return pl.pallas_call(
        kernel,
        out_shape=tuple((pltpu.HBM if spec is HBM else jax.ShapeDtypeStruct)(shape, dtype) for shape, dtype, spec in outs),
        in_specs=specs + [VMEM] * (len(args) - len(specs)),
        out_specs=tuple(spec for _, _, spec in outs),
        scratch_shapes=list(scratch),
        compiler_params=pltpu.CompilerParams(vmem_limit_bytes=vmem * 2**20),
        cost_estimate=pl.CostEstimate(flops=flops, bytes_accessed=nbytes, transcendentals=trans),
    )(*args)


def add(a, b):
    return (a.astype(F32) + b.astype(F32)).astype(BF)


def ring_gather(block):
    far = shifted(block, "z", 4)
    up = [block]
    down = [block]
    for _ in range(3):
        up.append(shifted(up[-1], "z", -1))
        down.append(shifted(down[-1], "z", 1))
    return up + [far] + down[:0:-1]


def near_step(rest):
    direct = [shifted(rest[k - 1], "z", k) for k in (4, 3, 5)]
    up, down = shifted(rest[1], "z", 1), shifted(rest[5], "z", -1)
    return direct, add(rest[0], up), add(rest[6], down)


def on_device(images, texts, log_temp, bias):
    temp = jnp.exp(log_temp[0])
    rows, width = images.shape
    n_plane = lax.axis_size(PLANE)
    half = ROWS * lax.axis_size("z")
    pooled = ROWS * n_plane
    (spread,) = local(
        spread_kernel, [((n_plane, rows, width), BF, HBM)], [texts],
        scratch=[pltpu.VMEM((rows, width), BF), pltpu.SemaphoreType.DMA((n_plane,))],
    )
    spread, images = lax.optimization_barrier((spread, images))
    ts = swapped(spread, WHOLE).reshape(pooled, width)
    (x,) = local(unit_kernel, [((rows, width), BF, VMEM)], [images])
    (xs,) = local(pack_kernel, [((half, width), BF, VMEM)], ring_gather(x))
    xo = shifted(xs, "core", 1)
    at_x, at_y = lax.axis_index("x"), lax.axis_index(("yh", "yl"))
    place = jnp.where(lax.axis_index("core") == 0, 4 * at_y + at_x, 4 * at_x + at_y).astype(jnp.int32).reshape(1)
    scal = jnp.stack([temp, bias[0]])
    unit_flops = 2 * half * pooled * width
    dxs, dxo, dy = local(
        pair_kernel,
        [((half, width), F32, HBM), ((half, width), BF, HBM), ((pooled, width), BF, HBM)],
        [place, scal, xs, xo, ts], smem=2, hbm=2,
        scratch=[
            pltpu.VMEM((2 * half, width), BF),
            pltpu.VMEM((pooled, 2 * half), BF),
            pltpu.VMEM((half, width), F32),
            pltpu.VMEM((half, width), BF),
            pltpu.VMEM((pooled, width), BF),
            pltpu.SemaphoreType.DMA((8,)),
        ],
        flops=6 * unit_flops, nbytes=9 * 2**20, trans=4 * half * pooled, vmem=24,
    )
    half_way = swapped(dy.reshape(4, 4 * rows, width), OUTER)
    other = shifted(dxo, "core", 1)
    own, rest = local(
        join_kernel, [((rows, width), F32, VMEM), ((half - rows, width), BF, VMEM)], [dxs, other],
        nbytes=5 * 2**20, vmem=16,
    )
    direct, up, down = near_step(rest.reshape(-1, rows, width))
    half_way, up, down = lax.optimization_barrier((half_way, up, down))
    (half_way,) = local(
        sum_kernel, [((4, rows, width), BF, HBM)], [half_way.reshape(4, 4, rows, width)], nbytes=3 * 2**20, vmem=16,
        scratch=[pltpu.VMEM((4, rows, width), BF), pltpu.SemaphoreType.DMA((4,))],
    )
    dyr = swapped(half_way, INNER)
    got = direct + [shifted(up, "z", 1), shifted(down, "z", -1)]
    (grad_images,) = local(finish_kernel, [((rows, width), F32, VMEM)], [scal, images, own] + got, smem=1)
    (grad_texts,) = local(finish_texts_kernel, [((rows, width), F32, VMEM)], [scal, texts, dyr], smem=1)
    return (grad_images, grad_texts)


def solution(mesh):
    fine = Mesh(mesh.devices.reshape(2, 4, 2, 2, 8), AXES)
    split = P(AXES, None)
    return jax.shard_map(
        on_device,
        mesh=fine,
        in_specs=(split, split, P(), P()),
        out_specs=(split, split),
        check_vma=False,
    )
```

```python
import jax
import jax.numpy as jnp
from jax import lax
from jax.experimental import pallas as pl
from jax.experimental.pallas import tpu as pltpu
from jax.sharding import Mesh, PartitionSpec as P

AXES = ("yh", "x", "core", "yl", "z")
PLANE = ("yh", "x", "yl")
BF = jnp.bfloat16
F32 = jnp.float32
LOG2E = 1.4426950408889634
ROWS = 64
NT = (((1,), (1,)), ((), ()))
TN = (((0,), (0,)), ((), ()))


def shifted(block, axis, distance):
    n = lax.axis_size(axis)
    return lax.ppermute(block, axis, [(i, (i + distance) % n) for i in range(n)])


def to_unit(raw):
    norm = jnp.sqrt(jnp.sum(raw * raw, axis=1, keepdims=True) + 1e-06)
    return (raw / norm, norm)


def from_unit(grad, unit, norm):
    return (grad - unit * jnp.sum(unit * grad, axis=1, keepdims=True)) / norm


def unit_rows(raw):
    norm = jnp.sqrt(jnp.sum(raw * raw, axis=1, keepdims=True) + 1e-06)
    return (raw / norm).astype(BF)


def spread_kernel(raw, out, unit, sems):
    unit[...] = unit_rows(raw[...])
    copies = [pltpu.make_async_copy(unit, out.at[k], sems.at[k]) for k in range(out.shape[0])]
    for copy in copies:
        copy.start()
    for copy in copies:
        copy.wait()


def unit_kernel(raw, out):
    out[...] = unit_rows(raw[...])


def pack_kernel(*refs):
    for k, block in enumerate(refs[:-1]):
        refs[-1][k * ROWS : (k + 1) * ROWS] = block[...]


def sigmoid(temp, offset, dots):
    return 1.0 / (1.0 + jnp.exp2(dots * (temp * -LOG2E) + offset * -LOG2E))


def pair_kernel(place, scal, xs, xo, ts, dxs, dxo, dy, x, held, mine, theirs, part, sems):
    temp = scal[0]
    offset = scal[1]
    half = xs.shape[0]
    pooled = ts.shape[0]
    wide = 512
    step = 256
    loads = [
        pltpu.make_async_copy(xs, x.at[0:half], sems.at[0]),
        pltpu.make_async_copy(xo, x.at[half : 2 * half], sems.at[1]),
    ]
    for copy in loads:
        copy.start()
    for h, copy in enumerate(loads):
        copy.wait()
        cols = slice(h * half, (h + 1) * half)
        for j in range(pooled // step):
            sl = pl.ds(j * step, step)
            dots = lax.dot_general(ts[sl], x[cols], NT, preferred_element_type=F32)
            held[sl, cols] = sigmoid(temp, offset, dots).astype(BF)
    at = pl.multiple_of(place[0] * ROWS, ROWS)
    dots = lax.dot_general(ts[pl.ds(at, ROWS)], x[0:ROWS], NT, preferred_element_type=F32)
    eye = lax.broadcasted_iota(jnp.int32, (ROWS, ROWS), 0) == lax.broadcasted_iota(
        jnp.int32, (ROWS, ROWS), 1
    )
    held[pl.ds(at, ROWS), 0:ROWS] = (sigmoid(temp, offset, dots) - eye.astype(F32)).astype(BF)
    copies = []

    def send(src, dst):
        copies.append(pltpu.make_async_copy(src, dst, sems.at[2 + len(copies)]))
        copies[-1].start()

    for h, (buf, out) in enumerate(((mine, dxs), (theirs, dxo))):
        for i in range(0, half, wide):
            cols = slice(h * half + i, h * half + i + wide)
            dots = lax.dot_general(held[:, cols], ts[...], TN, preferred_element_type=F32)
            buf[i : i + wide] = dots.astype(buf.dtype)
            send(buf.at[i : i + wide], out.at[i : i + wide])
    for j in range(0, pooled, step):
        part[j : j + step] = jnp.dot(held[j : j + step], x[...], preferred_element_type=F32).astype(BF)
        send(part.at[j : j + step], dy.at[j : j + step])
    for copy in copies:
        copy.wait()


def join_kernel(dxs, other, own, rest):
    own[...] = dxs[0:ROWS] + other[0:ROWS].astype(F32)
    rest[...] = (dxs[ROWS:] + other[ROWS:].astype(F32)).astype(BF)


def finish_kernel(scal, raw, *refs):
    total = refs[0][...].astype(F32)
    for part in refs[1:-1]:
        total += part[...].astype(F32)
    unit, norm = to_unit(raw[...])
    refs[-1][...] = from_unit(scal[0] * total, unit, norm)


def finish_texts_kernel(scal, raw, got, out):
    total = got[0].astype(F32)
    for k in range(1, got.shape[0]):
        total += got[k].astype(F32)
    unit, norm = to_unit(raw[...])
    out[...] = from_unit(scal[0] * total, unit, norm)


VMEM = pl.BlockSpec(memory_space=pltpu.VMEM)
SMEM = pl.BlockSpec(memory_space=pltpu.SMEM)
HBM = pl.BlockSpec(memory_space=pltpu.HBM)


def local(kernel, outs, args, smem=0, hbm=0, scratch=(), flops=0, nbytes=2**20, trans=0, vmem=8):
    specs = [SMEM] * smem + [HBM] * hbm
    return pl.pallas_call(
        kernel,
        out_shape=tuple((pltpu.HBM if spec is HBM else jax.ShapeDtypeStruct)(shape, dtype) for shape, dtype, spec in outs),
        in_specs=specs + [VMEM] * (len(args) - len(specs)),
        out_specs=tuple(spec for _, _, spec in outs),
        scratch_shapes=list(scratch),
        compiler_params=pltpu.CompilerParams(vmem_limit_bytes=vmem * 2**20),
        cost_estimate=pl.CostEstimate(flops=flops, bytes_accessed=nbytes, transcendentals=trans),
    )(*args)


def add(a, b):
    return (a.astype(F32) + b.astype(F32)).astype(BF)


def ring_gather(block):
    far = shifted(block, "z", 4)
    up = [block]
    down = [block]
    for _ in range(3):
        up.append(shifted(up[-1], "z", -1))
        down.append(shifted(down[-1], "z", 1))
    return up + [far] + down[:0:-1]


def near_reduce(rest):
    direct = [shifted(rest[k - 1], "z", k) for k in (4, 3, 5)]
    up, down = shifted(rest[1], "z", 1), shifted(rest[5], "z", -1)
    up, down = shifted(add(rest[0], up), "z", 1), shifted(add(rest[6], down), "z", -1)
    return direct + [up, down]


def on_device(images, texts, log_temp, bias):
    temp = jnp.exp(log_temp[0])
    rows, width = images.shape
    n_plane = lax.axis_size(PLANE)
    half = ROWS * lax.axis_size("z")
    pooled = ROWS * n_plane
    (spread,) = local(
        spread_kernel, [((n_plane, rows, width), BF, HBM)], [texts],
        scratch=[pltpu.VMEM((rows, width), BF), pltpu.SemaphoreType.DMA((n_plane,))],
    )
    spread, images = lax.optimization_barrier((spread, images))
    ts = lax.all_to_all(spread, PLANE, 0, 0, tiled=True).reshape(pooled, width)
    (x,) = local(unit_kernel, [((rows, width), BF, VMEM)], [images])
    (xs,) = local(pack_kernel, [((half, width), BF, VMEM)], ring_gather(x))
    xo = shifted(xs, "core", 1)
    place = lax.axis_index(PLANE).astype(jnp.int32).reshape(1)
    scal = jnp.stack([temp, bias[0]])
    unit_flops = 2 * half * pooled * width
    dxs, dxo, dy = local(
        pair_kernel,
        [((half, width), F32, HBM), ((half, width), BF, HBM), ((pooled, width), BF, HBM)],
        [place, scal, xs, xo, ts], smem=2, hbm=2,
        scratch=[
            pltpu.VMEM((2 * half, width), BF),
            pltpu.VMEM((pooled, 2 * half), BF),
            pltpu.VMEM((half, width), F32),
            pltpu.VMEM((half, width), BF),
            pltpu.VMEM((pooled, width), BF),
            pltpu.SemaphoreType.DMA((8,)),
        ],
        flops=6 * unit_flops, nbytes=9 * 2**20, trans=4 * half * pooled, vmem=24,
    )
    dyr = lax.all_to_all(dy.reshape(n_plane, rows, width), PLANE, 0, 0, tiled=True)
    other = shifted(dxo, "core", 1)
    own, rest = local(
        join_kernel, [((rows, width), F32, VMEM), ((half - rows, width), BF, VMEM)], [dxs, other],
        nbytes=5 * 2**20, vmem=16,
    )
    got = near_reduce(rest.reshape(-1, rows, width))
    (grad_images,) = local(finish_kernel, [((rows, width), F32, VMEM)], [scal, images, own] + got, smem=1)
    (grad_texts,) = local(finish_texts_kernel, [((rows, width), F32, VMEM)], [scal, texts, dyr], smem=1)
    return (grad_images, grad_texts)


def solution(mesh):
    fine = Mesh(mesh.devices.reshape(2, 4, 2, 2, 8), AXES)
    split = P(AXES, None)
    return jax.shard_map(
        on_device,
        mesh=fine,
        in_specs=(split, split, P(), P()),
        out_specs=(split, split),
        check_vma=False,
    )
```

```python
import jax
import jax.numpy as jnp
from jax import lax
from jax.experimental import pallas as pl
from jax.experimental.pallas import tpu as pltpu
from jax.sharding import Mesh, PartitionSpec as P

AXES = ("yh", "x", "core", "yl", "z")
PLANE = ("yh", "x", "yl")
BF = jnp.bfloat16
F32 = jnp.float32
LOG2E = 1.4426950408889634
ROWS = 64
NT = (((1,), (1,)), ((), ()))
TN = (((0,), (0,)), ((), ()))


def shifted(block, axis, distance):
    n = lax.axis_size(axis)
    return lax.ppermute(block, axis, [(i, (i + distance) % n) for i in range(n)])


def to_unit(raw):
    norm = jnp.sqrt(jnp.sum(raw * raw, axis=1, keepdims=True) + 1e-06)
    return (raw / norm, norm)


def from_unit(grad, unit, norm):
    return (grad - unit * jnp.sum(unit * grad, axis=1, keepdims=True)) / norm


def unit_rows(raw):
    norm = jnp.sqrt(jnp.sum(raw * raw, axis=1, keepdims=True) + 1e-06)
    return (raw / norm).astype(BF)


def spread_kernel(texts, out, raw, unit, sems):
    n = out.shape[0]
    load = pltpu.make_async_copy(texts, raw, sems.at[n])
    load.start()
    load.wait()
    unit[...] = unit_rows(raw[...])
    copies = [pltpu.make_async_copy(unit, out.at[k], sems.at[k]) for k in range(n)]
    for copy in copies:
        copy.start()
    for copy in copies:
        copy.wait()


def unit_kernel(raw, out):
    out[...] = unit_rows(raw[...])


def pack_kernel(*refs):
    for k, block in enumerate(refs[:-1]):
        refs[-1][k * ROWS : (k + 1) * ROWS] = block[...]


def sigmoid(temp, offset, dots):
    return 1.0 / (1.0 + jnp.exp2(dots * (temp * -LOG2E) + offset * -LOG2E))


def pair_kernel(place, scal, xs, xo, ts, dxs, dxo, dy, x, held, mine, theirs, part, sems):
    temp = scal[0]
    offset = scal[1]
    half = xs.shape[0]
    pooled = ts.shape[0]
    wide = 512
    step = 256
    loads = []
    for c in range(0, 2 * half, step):
        src = (xs if c < half else xo).at[c % half : c % half + step]
        loads.append(pltpu.make_async_copy(src, x.at[c : c + step], sems.at[len(loads)]))
        loads[-1].start()
    for c, load in enumerate(loads):
        load.wait()
        cols = slice(c * step, (c + 1) * step)
        for j in range(pooled // step):
            sl = pl.ds(j * step, step)
            dots = lax.dot_general(ts[sl], x[cols], NT, preferred_element_type=F32)
            held[sl, cols] = sigmoid(temp, offset, dots).astype(BF)
    at = pl.multiple_of(place[0] * ROWS, ROWS)
    dots = lax.dot_general(ts[pl.ds(at, ROWS)], x[0:ROWS], NT, preferred_element_type=F32)
    eye = lax.broadcasted_iota(jnp.int32, (ROWS, ROWS), 0) == lax.broadcasted_iota(
        jnp.int32, (ROWS, ROWS), 1
    )
    held[pl.ds(at, ROWS), 0:ROWS] = (sigmoid(temp, offset, dots) - eye.astype(F32)).astype(BF)
    copies = []

    def send(src, dst):
        copies.append(pltpu.make_async_copy(src, dst, sems.at[len(loads) + len(copies)]))
        copies[-1].start()

    for h, (buf, out) in enumerate(((mine, dxs), (theirs, dxo))):
        for i in range(0, half, wide):
            cols = slice(h * half + i, h * half + i + wide)
            dots = lax.dot_general(held[:, cols], ts[...], TN, preferred_element_type=F32)
            buf[i : i + wide] = dots.astype(buf.dtype)
            send(buf.at[i : i + wide], out.at[i : i + wide])
    for j, n in ((0, 256), (256, 256), (512, 256), (768, 128), (896, 128)):
        part[j : j + n] = jnp.dot(held[j : j + n], x[...], preferred_element_type=F32).astype(BF)
        send(part.at[j : j + n], dy.at[j : j + n])
    for copy in copies:
        copy.wait()


def join_kernel(dxs, other, own, rest):
    own[...] = dxs[0:ROWS] + other[0:ROWS].astype(F32)
    rest[...] = (dxs[ROWS:] + other[ROWS:].astype(F32)).astype(BF)


def finish_kernel(scal, raw, *refs):
    total = refs[0][...].astype(F32)
    for part in refs[1:-1]:
        total += part[...].astype(F32)
    unit, norm = to_unit(raw[...])
    refs[-1][...] = from_unit(scal[0] * total, unit, norm)


def finish_texts_kernel(scal, raw, got, out):
    total = got[0].astype(F32)
    for k in range(1, got.shape[0]):
        total += got[k].astype(F32)
    unit, norm = to_unit(raw[...])
    out[...] = from_unit(scal[0] * total, unit, norm)


VMEM = pl.BlockSpec(memory_space=pltpu.VMEM)
SMEM = pl.BlockSpec(memory_space=pltpu.SMEM)
HBM = pl.BlockSpec(memory_space=pltpu.HBM)


def local(kernel, outs, args, smem=0, hbm=0, scratch=(), flops=0, nbytes=2**20, trans=0, vmem=8):
    specs = [SMEM] * smem + [HBM] * hbm
    return pl.pallas_call(
        kernel,
        out_shape=tuple((pltpu.HBM if spec is HBM else jax.ShapeDtypeStruct)(shape, dtype) for shape, dtype, spec in outs),
        in_specs=specs + [VMEM] * (len(args) - len(specs)),
        out_specs=tuple(spec for _, _, spec in outs),
        scratch_shapes=list(scratch),
        compiler_params=pltpu.CompilerParams(vmem_limit_bytes=vmem * 2**20),
        cost_estimate=pl.CostEstimate(flops=flops, bytes_accessed=nbytes, transcendentals=trans),
    )(*args)


def add(a, b):
    return (a.astype(F32) + b.astype(F32)).astype(BF)


def ring_gather(block):
    far = shifted(block, "z", 4)
    up = [block]
    down = [block]
    for _ in range(3):
        up.append(shifted(up[-1], "z", -1))
        down.append(shifted(down[-1], "z", 1))
    return up + [far] + down[:0:-1]


def near_reduce(rest):
    direct = [shifted(rest[k - 1], "z", k) for k in (4, 3, 5)]
    up, down = shifted(rest[1], "z", 1), shifted(rest[5], "z", -1)
    up, down = shifted(add(rest[0], up), "z", 1), shifted(add(rest[6], down), "z", -1)
    return direct + [up, down]


def on_device(images, texts, log_temp, bias):
    temp = jnp.exp(log_temp[0])
    rows, width = images.shape
    n_plane = lax.axis_size(PLANE)
    half = ROWS * lax.axis_size("z")
    pooled = ROWS * n_plane
    (spread,) = local(
        spread_kernel, [((n_plane, rows, width), BF, HBM)], [texts], hbm=1,
        scratch=[
            pltpu.VMEM((rows, width), F32),
            pltpu.VMEM((rows, width), BF),
            pltpu.SemaphoreType.DMA((n_plane + 1,)),
        ],
    )
    spread, images = lax.optimization_barrier((spread, images))
    ts = lax.all_to_all(spread, PLANE, 0, 0, tiled=True).reshape(pooled, width)
    (x,) = local(unit_kernel, [((rows, width), BF, VMEM)], [images])
    (xs,) = local(pack_kernel, [((half, width), BF, VMEM)], ring_gather(x))
    xo = shifted(xs, "core", 1)
    place = lax.axis_index(PLANE).astype(jnp.int32).reshape(1)
    scal = jnp.stack([temp, bias[0]])
    unit_flops = 2 * half * pooled * width
    dxs, dxo, dy = local(
        pair_kernel,
        [((half, width), F32, HBM), ((half, width), BF, HBM), ((pooled, width), BF, HBM)],
        [place, scal, xs, xo, ts], smem=2, hbm=2,
        scratch=[
            pltpu.VMEM((2 * half, width), BF),
            pltpu.VMEM((pooled, 2 * half), BF),
            pltpu.VMEM((half, width), F32),
            pltpu.VMEM((half, width), BF),
            pltpu.VMEM((pooled, width), BF),
            pltpu.SemaphoreType.DMA((11,)),
        ],
        flops=6 * unit_flops, nbytes=9 * 2**20, trans=4 * half * pooled, vmem=24,
    )
    dyr = lax.all_to_all(dy.reshape(n_plane, rows, width), PLANE, 0, 0, tiled=True)
    other = shifted(dxo, "core", 1)
    own, rest = local(
        join_kernel, [((rows, width), F32, VMEM), ((half - rows, width), BF, VMEM)], [dxs, other],
        nbytes=5 * 2**20, vmem=16,
    )
    got = near_reduce(rest.reshape(-1, rows, width))
    (grad_images,) = local(finish_kernel, [((rows, width), F32, VMEM)], [scal, images, own] + got, smem=1)
    (grad_texts,) = local(finish_texts_kernel, [((rows, width), F32, VMEM)], [scal, texts, dyr], smem=1)
    return (grad_images, grad_texts)


def solution(mesh):
    fine = Mesh(mesh.devices.reshape(2, 4, 2, 2, 8), AXES)
    split = P(AXES, None)
    return jax.shard_map(
        on_device,
        mesh=fine,
        in_specs=(split, split, P(), P()),
        out_specs=(split, split),
        check_vma=False,
    )
```

```python
import jax
import jax.numpy as jnp
from jax import lax
from jax.experimental import pallas as pl
from jax.experimental.pallas import tpu as pltpu
from jax.sharding import Mesh, PartitionSpec as P

AXES = ("yh", "x", "core", "yl", "z")
PLANE = ("yh", "x", "yl")
BF = jnp.bfloat16
F32 = jnp.float32
LOG2E = 1.4426950408889634
ROWS = 64
NT = (((1,), (1,)), ((), ()))
TN = (((0,), (0,)), ((), ()))


def shifted(block, axis, distance):
    n = lax.axis_size(axis)
    return lax.ppermute(block, axis, [(i, (i + distance) % n) for i in range(n)])


def to_unit(raw):
    norm = jnp.sqrt(jnp.sum(raw * raw, axis=1, keepdims=True) + 1e-06)
    return (raw / norm, norm)


def from_unit(grad, unit, norm):
    return (grad - unit * jnp.sum(unit * grad, axis=1, keepdims=True)) / norm


def unit_rows(raw):
    norm = jnp.sqrt(jnp.sum(raw * raw, axis=1, keepdims=True) + 1e-06)
    return (raw / norm).astype(BF)


def spread_kernel(texts, out, raw, unit, sems):
    n = out.shape[0]
    load = pltpu.make_async_copy(texts, raw, sems.at[n])
    load.start()
    load.wait()
    unit[...] = unit_rows(raw[...])
    copies = [pltpu.make_async_copy(unit, out.at[k], sems.at[k]) for k in range(n)]
    for copy in copies:
        copy.start()
    for copy in copies:
        copy.wait()


def unit_kernel(images, out, raw, sem):
    load = pltpu.make_async_copy(images, raw, sem)
    load.start()
    load.wait()
    out[...] = unit_rows(raw[...])


def pack_kernel(*refs):
    for k, block in enumerate(refs[:-1]):
        refs[-1][k * ROWS : (k + 1) * ROWS] = block[...]


def sigmoid(temp, offset, dots):
    return 1.0 / (1.0 + jnp.exp2(dots * (temp * -LOG2E) + offset * -LOG2E))


def pair_kernel(place, scal, xs, xo, ts, dxs, dxo, dy, x, held, mine, theirs, part, sems):
    temp = scal[0]
    offset = scal[1]
    half = xs.shape[0]
    pooled = ts.shape[0]
    wide = 512
    step = 256
    loads = [
        pltpu.make_async_copy(xs, x.at[0:half], sems.at[0]),
        pltpu.make_async_copy(xo, x.at[half : 2 * half], sems.at[1]),
    ]
    for copy in loads:
        copy.start()
    for h, copy in enumerate(loads):
        copy.wait()
        cols = slice(h * half, (h + 1) * half)
        for j in range(pooled // step):
            sl = pl.ds(j * step, step)
            dots = lax.dot_general(ts[sl], x[cols], NT, preferred_element_type=F32)
            held[sl, cols] = sigmoid(temp, offset, dots).astype(BF)
    at = pl.multiple_of(place[0] * ROWS, ROWS)
    dots = lax.dot_general(ts[pl.ds(at, ROWS)], x[0:ROWS], NT, preferred_element_type=F32)
    eye = lax.broadcasted_iota(jnp.int32, (ROWS, ROWS), 0) == lax.broadcasted_iota(
        jnp.int32, (ROWS, ROWS), 1
    )
    held[pl.ds(at, ROWS), 0:ROWS] = (sigmoid(temp, offset, dots) - eye.astype(F32)).astype(BF)
    copies = []

    def send(src, dst):
        copies.append(pltpu.make_async_copy(src, dst, sems.at[2 + len(copies)]))
        copies[-1].start()

    for h, (buf, out) in enumerate(((mine, dxs), (theirs, dxo))):
        for i in range(0, half, wide):
            cols = slice(h * half + i, h * half + i + wide)
            dots = lax.dot_general(held[:, cols], ts[...], TN, preferred_element_type=F32)
            buf[i : i + wide] = dots.astype(buf.dtype)
            send(buf.at[i : i + wide], out.at[i : i + wide])
    for j in range(0, pooled, step):
        part[j : j + step] = jnp.dot(held[j : j + step], x[...], preferred_element_type=F32).astype(BF)
        send(part.at[j : j + step], dy.at[j : j + step])
    for copy in copies:
        copy.wait()


def join_kernel(dxs, other, own, rest):
    own[...] = dxs[0:ROWS] + other[0:ROWS].astype(F32)
    rest[...] = (dxs[ROWS:] + other[ROWS:].astype(F32)).astype(BF)


def finish_kernel(scal, raw, *refs):
    total = refs[0][...].astype(F32)
    for part in refs[1:-1]:
        total += part[...].astype(F32)
    unit, norm = to_unit(raw[...])
    refs[-1][...] = from_unit(scal[0] * total, unit, norm)


def finish_texts_kernel(scal, raw, got, out, part, sems):
    copies = []
    step = 16
    for i in range(0, ROWS, step):
        sl = slice(i, i + step)
        total = got[0, sl].astype(F32)
        for k in range(1, got.shape[0]):
            total += got[k, sl].astype(F32)
        unit, norm = to_unit(raw[sl])
        part[sl] = from_unit(scal[0] * total, unit, norm)
        copies.append(pltpu.make_async_copy(part.at[sl], out.at[sl], sems.at[len(copies)]))
        copies[-1].start()
    for copy in copies:
        copy.wait()


VMEM = pl.BlockSpec(memory_space=pltpu.VMEM)
SMEM = pl.BlockSpec(memory_space=pltpu.SMEM)
HBM = pl.BlockSpec(memory_space=pltpu.HBM)


def local(kernel, outs, args, smem=0, hbm=0, scratch=(), flops=0, nbytes=2**20, trans=0, vmem=8):
    specs = [SMEM] * smem + [HBM] * hbm
    return pl.pallas_call(
        kernel,
        out_shape=tuple((pltpu.HBM if spec is HBM else jax.ShapeDtypeStruct)(shape, dtype) for shape, dtype, spec in outs),
        in_specs=specs + [VMEM] * (len(args) - len(specs)),
        out_specs=tuple(spec for _, _, spec in outs),
        scratch_shapes=list(scratch),
        compiler_params=pltpu.CompilerParams(vmem_limit_bytes=vmem * 2**20),
        cost_estimate=pl.CostEstimate(flops=flops, bytes_accessed=nbytes, transcendentals=trans),
    )(*args)


def add(a, b):
    return (a.astype(F32) + b.astype(F32)).astype(BF)


def ring_gather(block):
    far = shifted(block, "z", 4)
    up = [block]
    down = [block]
    for _ in range(3):
        up.append(shifted(up[-1], "z", -1))
        down.append(shifted(down[-1], "z", 1))
    return up + [far] + down[:0:-1]


def near_reduce(rest):
    direct = [shifted(rest[k - 1], "z", k) for k in (4, 3, 5)]
    up, down = shifted(rest[1], "z", 1), shifted(rest[5], "z", -1)
    up, down = shifted(add(rest[0], up), "z", 1), shifted(add(rest[6], down), "z", -1)
    return direct + [up, down]


def on_device(images, texts, log_temp, bias):
    temp = jnp.exp(log_temp[0])
    rows, width = images.shape
    n_plane = lax.axis_size(PLANE)
    half = ROWS * lax.axis_size("z")
    pooled = ROWS * n_plane
    (spread,) = local(
        spread_kernel, [((n_plane, rows, width), BF, HBM)], [texts], hbm=1,
        scratch=[
            pltpu.VMEM((rows, width), F32),
            pltpu.VMEM((rows, width), BF),
            pltpu.SemaphoreType.DMA((n_plane + 1,)),
        ],
    )
    spread, images = lax.optimization_barrier((spread, images))
    ts = lax.all_to_all(spread, PLANE, 0, 0, tiled=True).reshape(pooled, width)
    (x,) = local(
        unit_kernel, [((rows, width), BF, VMEM)], [images], hbm=1,
        scratch=[pltpu.VMEM((rows, width), F32), pltpu.SemaphoreType.DMA],
    )
    (xs,) = local(pack_kernel, [((half, width), BF, VMEM)], ring_gather(x))
    xo = shifted(xs, "core", 1)
    place = lax.axis_index(PLANE).astype(jnp.int32).reshape(1)
    scal = jnp.stack([temp, bias[0]])
    unit_flops = 2 * half * pooled * width
    dxs, dxo, dy = local(
        pair_kernel,
        [((half, width), F32, HBM), ((half, width), BF, HBM), ((pooled, width), BF, HBM)],
        [place, scal, xs, xo, ts], smem=2, hbm=2,
        scratch=[
            pltpu.VMEM((2 * half, width), BF),
            pltpu.VMEM((pooled, 2 * half), BF),
            pltpu.VMEM((half, width), F32),
            pltpu.VMEM((half, width), BF),
            pltpu.VMEM((pooled, width), BF),
            pltpu.SemaphoreType.DMA((8,)),
        ],
        flops=6 * unit_flops, nbytes=9 * 2**20, trans=4 * half * pooled, vmem=24,
    )
    dyr = lax.all_to_all(dy.reshape(n_plane, rows, width), PLANE, 0, 0, tiled=True)
    other = shifted(dxo, "core", 1)
    own, rest = local(
        join_kernel, [((rows, width), F32, VMEM), ((half - rows, width), BF, VMEM)], [dxs, other],
        nbytes=5 * 2**20, vmem=16,
    )
    got = near_reduce(rest.reshape(-1, rows, width))
    (grad_images,) = local(finish_kernel, [((rows, width), F32, VMEM)], [scal, images, own] + got, smem=1)
    (grad_texts,) = local(
        finish_texts_kernel, [((rows, width), F32, HBM)], [scal, texts, dyr], smem=1,
        scratch=[pltpu.VMEM((rows, width), F32), pltpu.SemaphoreType.DMA((4,))],
    )
    return (grad_images, grad_texts)


def solution(mesh):
    fine = Mesh(mesh.devices.reshape(2, 4, 2, 2, 8), AXES)
    split = P(AXES, None)
    return jax.shard_map(
        on_device,
        mesh=fine,
        in_specs=(split, split, P(), P()),
        out_specs=(split, split),
        check_vma=False,
    )
```

```python
import jax
import jax.numpy as jnp
from jax import lax
from jax.experimental import pallas as pl
from jax.experimental.pallas import tpu as pltpu
from jax.sharding import Mesh, PartitionSpec as P

AXES = ("yh", "x", "core", "yl", "z")
PLANE = ("yh", "x", "yl")
BF = jnp.bfloat16
F32 = jnp.float32
LOG2E = 1.4426950408889634
ROWS = 64
NT = (((1,), (1,)), ((), ()))
TN = (((0,), (0,)), ((), ()))


def shifted(block, axis, distance):
    n = lax.axis_size(axis)
    return lax.ppermute(block, axis, [(i, (i + distance) % n) for i in range(n)])


def to_unit(raw):
    norm = jnp.sqrt(jnp.sum(raw * raw, axis=1, keepdims=True) + 1e-06)
    return (raw / norm, norm)


def from_unit(grad, unit, norm):
    return (grad - unit * jnp.sum(unit * grad, axis=1, keepdims=True)) / norm


def unit_rows(raw):
    norm = jnp.sqrt(jnp.sum(raw * raw, axis=1, keepdims=True) + 1e-06)
    return (raw / norm).astype(BF)


def spread_kernel(texts, out, raw, unit, sems):
    n = out.shape[0]
    load = pltpu.make_async_copy(texts, raw, sems.at[n])
    load.start()
    load.wait()
    unit[...] = unit_rows(raw[...])
    copies = [pltpu.make_async_copy(unit, out.at[k], sems.at[k]) for k in range(n)]
    for copy in copies:
        copy.start()
    for copy in copies:
        copy.wait()


def unit_kernel(images, out, raw, sem):
    load = pltpu.make_async_copy(images, raw, sem)
    load.start()
    load.wait()
    out[...] = unit_rows(raw[...])


def pack_kernel(*refs):
    for k, block in enumerate(refs[:-1]):
        refs[-1][k * ROWS : (k + 1) * ROWS] = block[...]


def sigmoid(temp, offset, dots):
    return 1.0 / (1.0 + jnp.exp2(dots * (temp * -LOG2E) + offset * -LOG2E))


def pair_kernel(place, scal, xs, xo, ts, dxs, dxo, dy, x, held, mine, theirs, part, sems):
    temp = scal[0]
    offset = scal[1]
    half = xs.shape[0]
    pooled = ts.shape[0]
    wide = 512
    step = 256
    loads = [
        pltpu.make_async_copy(xs, x.at[0:half], sems.at[0]),
        pltpu.make_async_copy(xo, x.at[half : 2 * half], sems.at[1]),
    ]
    for copy in loads:
        copy.start()
    for h, copy in enumerate(loads):
        copy.wait()
        cols = slice(h * half, (h + 1) * half)
        for j in range(pooled // step):
            sl = pl.ds(j * step, step)
            dots = lax.dot_general(ts[sl], x[cols], NT, preferred_element_type=F32)
            held[sl, cols] = sigmoid(temp, offset, dots).astype(BF)
    at = pl.multiple_of(place[0] * ROWS, ROWS)
    dots = lax.dot_general(ts[pl.ds(at, ROWS)], x[0:ROWS], NT, preferred_element_type=F32)
    eye = lax.broadcasted_iota(jnp.int32, (ROWS, ROWS), 0) == lax.broadcasted_iota(
        jnp.int32, (ROWS, ROWS), 1
    )
    held[pl.ds(at, ROWS), 0:ROWS] = (sigmoid(temp, offset, dots) - eye.astype(F32)).astype(BF)
    copies = []

    def send(src, dst):
        copies.append(pltpu.make_async_copy(src, dst, sems.at[2 + len(copies)]))
        copies[-1].start()

    for h, (buf, out) in enumerate(((mine, dxs), (theirs, dxo))):
        for i in range(0, half, wide):
            cols = slice(h * half + i, h * half + i + wide)
            dots = lax.dot_general(held[:, cols], ts[...], TN, preferred_element_type=F32)
            buf[i : i + wide] = dots.astype(buf.dtype)
            send(buf.at[i : i + wide], out.at[i : i + wide])
    for j in range(0, pooled, step):
        part[j : j + step] = jnp.dot(held[j : j + step], x[...], preferred_element_type=F32).astype(BF)
        send(part.at[j : j + step], dy.at[j : j + step])
    for copy in copies:
        copy.wait()


def join_kernel(dxs, other, own, rest):
    own[...] = dxs[0:ROWS] + other[0:ROWS].astype(F32)
    rest[...] = (dxs[ROWS:] + other[ROWS:].astype(F32)).astype(BF)


def finish_kernel(scal, raw, *refs):
    total = refs[0][...].astype(F32)
    for part in refs[1:-1]:
        total += part[...].astype(F32)
    unit, norm = to_unit(raw[...])
    refs[-1][...] = from_unit(scal[0] * total, unit, norm)


def finish_texts_kernel(scal, raw, got, out, part, sems):
    copies = []
    step = 16
    for i in range(0, ROWS, step):
        sl = slice(i, i + step)
        total = got[0, sl].astype(F32)
        for k in range(1, got.shape[0]):
            total += got[k, sl].astype(F32)
        unit, norm = to_unit(raw[sl])
        part[sl] = from_unit(scal[0] * total, unit, norm)
        copies.append(pltpu.make_async_copy(part.at[sl], out.at[sl], sems.at[len(copies)]))
        copies[-1].start()
    for copy in copies:
        copy.wait()


VMEM = pl.BlockSpec(memory_space=pltpu.VMEM)
SMEM = pl.BlockSpec(memory_space=pltpu.SMEM)
HBM = pl.BlockSpec(memory_space=pltpu.HBM)


def local(kernel, outs, args, smem=0, hbm=0, scratch=(), flops=0, nbytes=2**20, trans=0, vmem=8):
    specs = [SMEM] * smem + [HBM] * hbm
    return pl.pallas_call(
        kernel,
        out_shape=tuple((pltpu.HBM if spec is HBM else jax.ShapeDtypeStruct)(shape, dtype) for shape, dtype, spec in outs),
        in_specs=specs + [VMEM] * (len(args) - len(specs)),
        out_specs=tuple(spec for _, _, spec in outs),
        scratch_shapes=list(scratch),
        compiler_params=pltpu.CompilerParams(vmem_limit_bytes=int(vmem * 2**20)),
        cost_estimate=pl.CostEstimate(flops=flops, bytes_accessed=nbytes, transcendentals=trans),
    )(*args)


def add(a, b):
    return (a.astype(F32) + b.astype(F32)).astype(BF)


def ring_gather(block):
    far = shifted(block, "z", 4)
    up = [block]
    down = [block]
    for _ in range(3):
        up.append(shifted(up[-1], "z", -1))
        down.append(shifted(down[-1], "z", 1))
    return up + [far] + down[:0:-1]


def near_reduce(rest):
    direct = [shifted(rest[k - 1], "z", k) for k in (4, 3, 5)]
    up, down = shifted(rest[1], "z", 1), shifted(rest[5], "z", -1)
    up, down = shifted(add(rest[0], up), "z", 1), shifted(add(rest[6], down), "z", -1)
    return direct + [up, down]


def on_device(images, texts, log_temp, bias):
    temp = jnp.exp(log_temp[0])
    rows, width = images.shape
    n_plane = lax.axis_size(PLANE)
    half = ROWS * lax.axis_size("z")
    pooled = ROWS * n_plane
    (spread,) = local(
        spread_kernel, [((n_plane, rows, width), BF, HBM)], [texts], hbm=1, vmem=60.5,
        scratch=[
            pltpu.VMEM((rows, width), F32),
            pltpu.VMEM((rows, width), BF),
            pltpu.SemaphoreType.DMA((n_plane + 1,)),
        ],
    )
    spread, images = lax.optimization_barrier((spread, images))
    ts = lax.all_to_all(spread, PLANE, 0, 0, tiled=True).reshape(pooled, width)
    (x,) = local(
        unit_kernel, [((rows, width), BF, VMEM)], [images], hbm=1,
        scratch=[pltpu.VMEM((rows, width), F32), pltpu.SemaphoreType.DMA],
    )
    (xs,) = local(pack_kernel, [((half, width), BF, VMEM)], ring_gather(x))
    xo = shifted(xs, "core", 1)
    place = lax.axis_index(PLANE).astype(jnp.int32).reshape(1)
    scal = jnp.stack([temp, bias[0]])
    unit_flops = 2 * half * pooled * width
    dxs, dxo, dy = local(
        pair_kernel,
        [((half, width), F32, HBM), ((half, width), BF, HBM), ((pooled, width), BF, HBM)],
        [place, scal, xs, xo, ts], smem=2, hbm=2,
        scratch=[
            pltpu.VMEM((2 * half, width), BF),
            pltpu.VMEM((pooled, 2 * half), BF),
            pltpu.VMEM((half, width), F32),
            pltpu.VMEM((half, width), BF),
            pltpu.VMEM((pooled, width), BF),
            pltpu.SemaphoreType.DMA((8,)),
        ],
        flops=6 * unit_flops, nbytes=9 * 2**20, trans=4 * half * pooled, vmem=24,
    )
    dyr = lax.all_to_all(dy.reshape(n_plane, rows, width), PLANE, 0, 0, tiled=True)
    other = shifted(dxo, "core", 1)
    own, rest = local(
        join_kernel, [((rows, width), F32, VMEM), ((half - rows, width), BF, VMEM)], [dxs, other],
        nbytes=5 * 2**20, vmem=16,
    )
    got = near_reduce(rest.reshape(-1, rows, width))
    (grad_images,) = local(finish_kernel, [((rows, width), F32, VMEM)], [scal, images, own] + got, smem=1)
    (grad_texts,) = local(
        finish_texts_kernel, [((rows, width), F32, HBM)], [scal, texts, dyr], smem=1,
        scratch=[pltpu.VMEM((rows, width), F32), pltpu.SemaphoreType.DMA((4,))],
    )
    return (grad_images, grad_texts)


def solution(mesh):
    fine = Mesh(mesh.devices.reshape(2, 4, 2, 2, 8), AXES)
    split = P(AXES, None)
    return jax.shard_map(
        on_device,
        mesh=fine,
        in_specs=(split, split, P(), P()),
        out_specs=(split, split),
        check_vma=False,
    )
```

```python
import jax
import jax.numpy as jnp
from jax import lax
from jax.experimental import pallas as pl
from jax.experimental.pallas import tpu as pltpu
from jax.sharding import Mesh, PartitionSpec as P

AXES = ("yh", "x", "core", "yl", "z")
PLANE = ("yh", "x", "yl")
BF = jnp.bfloat16
F32 = jnp.float32
LOG2E = 1.4426950408889634
ROWS = 64
NT = (((1,), (1,)), ((), ()))
TN = (((0,), (0,)), ((), ()))


def shifted(block, axis, distance):
    n = lax.axis_size(axis)
    return lax.ppermute(block, axis, [(i, (i + distance) % n) for i in range(n)])


def to_unit(raw):
    norm = jnp.sqrt(jnp.sum(raw * raw, axis=1, keepdims=True) + 1e-06)
    return (raw / norm, norm)


def from_unit(grad, unit, norm):
    return (grad - unit * jnp.sum(unit * grad, axis=1, keepdims=True)) / norm


def unit_rows(raw):
    norm = jnp.sqrt(jnp.sum(raw * raw, axis=1, keepdims=True) + 1e-06)
    return (raw / norm).astype(BF)


def spread_kernel(texts, out, raw, unit, sems):
    n = out.shape[0]
    step = 16
    loads = []
    for i in range(0, ROWS, step):
        sl = slice(i, i + step)
        loads.append(pltpu.make_async_copy(texts.at[sl], raw.at[sl], sems.at[n + len(loads)]))
        loads[-1].start()
    for i, load in enumerate(loads):
        load.wait()
        sl = slice(i * step, (i + 1) * step)
        unit[sl] = unit_rows(raw[sl])
    copies = [pltpu.make_async_copy(unit, out.at[k], sems.at[k]) for k in range(n)]
    for copy in copies:
        copy.start()
    for copy in copies:
        copy.wait()


def unit_kernel(images, out, raw, sem):
    load = pltpu.make_async_copy(images, raw, sem)
    load.start()
    load.wait()
    out[...] = unit_rows(raw[...])


def pack_kernel(*refs):
    for k, block in enumerate(refs[:-1]):
        refs[-1][k * ROWS : (k + 1) * ROWS] = block[...]


def sigmoid(temp, offset, dots):
    return 1.0 / (1.0 + jnp.exp2(dots * (temp * -LOG2E) + offset * -LOG2E))


def pair_kernel(place, scal, xs, xo, ts, coeff, kept, dxo, dy, x, held, theirs, part, sems):
    temp = scal[0]
    offset = scal[1]
    half = xs.shape[0]
    pooled = ts.shape[0]
    wide = 512
    step = 256
    loads = [
        pltpu.make_async_copy(xs, x.at[0:half], sems.at[0]),
        pltpu.make_async_copy(xo, x.at[half : 2 * half], sems.at[1]),
    ]
    for copy in loads:
        copy.start()
    for h, copy in enumerate(loads):
        copy.wait()
        cols = slice(h * half, (h + 1) * half)
        for j in range(pooled // step):
            sl = pl.ds(j * step, step)
            dots = lax.dot_general(ts[sl], x[cols], NT, preferred_element_type=F32)
            held[sl, cols] = sigmoid(temp, offset, dots).astype(BF)
    at = pl.multiple_of(place[0] * ROWS, ROWS)
    dots = lax.dot_general(ts[pl.ds(at, ROWS)], x[0:ROWS], NT, preferred_element_type=F32)
    eye = lax.broadcasted_iota(jnp.int32, (ROWS, ROWS), 0) == lax.broadcasted_iota(
        jnp.int32, (ROWS, ROWS), 1
    )
    held[pl.ds(at, ROWS), 0:ROWS] = (sigmoid(temp, offset, dots) - eye.astype(F32)).astype(BF)
    copies = []

    def send(src, dst):
        copies.append(pltpu.make_async_copy(src, dst, sems.at[2 + len(copies)]))
        copies[-1].start()

    send(ts, kept)
    send(held.at[:, 0:half], coeff)
    for i in range(0, half, wide):
        cols = slice(half + i, half + i + wide)
        dots = lax.dot_general(held[:, cols], ts[...], TN, preferred_element_type=F32)
        theirs[i : i + wide] = dots.astype(BF)
        send(theirs.at[i : i + wide], dxo.at[i : i + wide])
    for j in range(0, pooled, step):
        part[j : j + step] = jnp.dot(held[j : j + step], x[...], preferred_element_type=F32).astype(BF)
        send(part.at[j : j + step], dy.at[j : j + step])
    for copy in copies:
        copy.wait()


def join_kernel(coeff, kept, other, own, rest, held, ts, theirs, mine, sums, sems):
    pooled, half = coeff.shape
    step = 256
    pairs = [(coeff.at[j : j + step], held.at[j : j + step]) for j in range(0, pooled, step)]
    pairs += [(kept.at[j : j + step], ts.at[j : j + step]) for j in range(0, pooled, step)]
    pairs += [(other, theirs)]
    loads = [pltpu.make_async_copy(src, dst, sems.at[k]) for k, (src, dst) in enumerate(pairs)]
    for copy in loads:
        copy.start()
    for copy in loads:
        copy.wait()
    copies = []
    for i in range(0, half, step):
        part = lax.dot_general(held[:, i : i + step], ts[...], TN, preferred_element_type=F32)
        part += theirs[i : i + step].astype(F32)
        if i == 0:
            mine[...] = part[0:ROWS]
            sums[0 : step - ROWS] = part[ROWS:].astype(BF)
            sl = slice(0, step - ROWS)
            copies.append(pltpu.make_async_copy(mine, own, sems.at[len(loads)]))
            copies[-1].start()
        else:
            sl = slice(i - ROWS, i - ROWS + step)
            sums[sl] = part.astype(BF)
        copies.append(pltpu.make_async_copy(sums.at[sl], rest.at[sl], sems.at[len(loads) + len(copies)]))
        copies[-1].start()
    for copy in copies:
        copy.wait()


def finish_kernel(scal, raw, *refs):
    total = refs[0][...].astype(F32)
    for part in refs[1:-1]:
        total += part[...].astype(F32)
    unit, norm = to_unit(raw[...])
    refs[-1][...] = from_unit(scal[0] * total, unit, norm)


def finish_texts_kernel(scal, raw, got, out, part, sems):
    copies = []
    step = 16
    for i in range(0, ROWS, step):
        sl = slice(i, i + step)
        total = got[0, sl].astype(F32)
        for k in range(1, got.shape[0]):
            total += got[k, sl].astype(F32)
        unit, norm = to_unit(raw[sl])
        part[sl] = from_unit(scal[0] * total, unit, norm)
        copies.append(pltpu.make_async_copy(part.at[sl], out.at[sl], sems.at[len(copies)]))
        copies[-1].start()
    for copy in copies:
        copy.wait()


VMEM = pl.BlockSpec(memory_space=pltpu.VMEM)
SMEM = pl.BlockSpec(memory_space=pltpu.SMEM)
HBM = pl.BlockSpec(memory_space=pltpu.HBM)


def local(kernel, outs, args, smem=0, hbm=0, scratch=(), flops=0, nbytes=2**20, trans=0, vmem=8):
    specs = [SMEM] * smem + [HBM] * hbm
    return pl.pallas_call(
        kernel,
        out_shape=tuple((pltpu.HBM if spec is HBM else jax.ShapeDtypeStruct)(shape, dtype) for shape, dtype, spec in outs),
        in_specs=specs + [VMEM] * (len(args) - len(specs)),
        out_specs=tuple(spec for _, _, spec in outs),
        scratch_shapes=list(scratch),
        compiler_params=pltpu.CompilerParams(vmem_limit_bytes=int(vmem * 2**20)),
        cost_estimate=pl.CostEstimate(flops=flops, bytes_accessed=nbytes, transcendentals=trans),
    )(*args)


def add(a, b):
    return (a.astype(F32) + b.astype(F32)).astype(BF)


def ring_gather(block):
    far = shifted(block, "z", 4)
    up = [block]
    down = [block]
    for _ in range(3):
        up.append(shifted(up[-1], "z", -1))
        down.append(shifted(down[-1], "z", 1))
    return up + [far] + down[:0:-1]


def near_reduce(rest):
    direct = [shifted(rest[k - 1], "z", k) for k in (4, 3, 5)]
    up, down = shifted(rest[1], "z", 1), shifted(rest[5], "z", -1)
    up, down = shifted(add(rest[0], up), "z", 1), shifted(add(rest[6], down), "z", -1)
    return direct + [up, down]


def on_device(images, texts, log_temp, bias):
    temp = jnp.exp(log_temp[0])
    rows, width = images.shape
    n_plane = lax.axis_size(PLANE)
    half = ROWS * lax.axis_size("z")
    pooled = ROWS * n_plane
    (spread,) = local(
        spread_kernel, [((n_plane, rows, width), BF, HBM)], [texts], hbm=1, vmem=60.5,
        scratch=[
            pltpu.VMEM((rows, width), F32),
            pltpu.VMEM((rows, width), BF),
            pltpu.SemaphoreType.DMA((n_plane + 4,)),
        ],
    )
    spread, images = lax.optimization_barrier((spread, images))
    ts = lax.all_to_all(spread, PLANE, 0, 0, tiled=True).reshape(pooled, width)
    (x,) = local(
        unit_kernel, [((rows, width), BF, VMEM)], [images], hbm=1,
        scratch=[pltpu.VMEM((rows, width), F32), pltpu.SemaphoreType.DMA],
    )
    (xs,) = local(pack_kernel, [((half, width), BF, VMEM)], ring_gather(x))
    xo = shifted(xs, "core", 1)
    place = lax.axis_index(PLANE).astype(jnp.int32).reshape(1)
    scal = jnp.stack([temp, bias[0]])
    unit_flops = 2 * half * pooled * width
    coeff, kept, dxo, dy = local(
        pair_kernel,
        [((pooled, half), BF, HBM), ((pooled, width), BF, HBM), ((half, width), BF, HBM), ((pooled, width), BF, HBM)],
        [place, scal, xs, xo, ts], smem=2, hbm=2,
        scratch=[
            pltpu.VMEM((2 * half, width), BF),
            pltpu.VMEM((pooled, 2 * half), BF),
            pltpu.VMEM((half, width), BF),
            pltpu.VMEM((pooled, width), BF),
            pltpu.SemaphoreType.DMA((9,)),
        ],
        flops=5 * unit_flops, nbytes=9 * 2**20, trans=4 * half * pooled, vmem=24,
    )
    dyr = lax.all_to_all(dy.reshape(n_plane, rows, width), PLANE, 0, 0, tiled=True)
    other = shifted(dxo, "core", 1)
    own, rest = local(
        join_kernel, [((rows, width), F32, HBM), ((half - rows, width), BF, HBM)], [coeff, kept, other], hbm=3,
        scratch=[
            pltpu.VMEM((pooled, half), BF),
            pltpu.VMEM((pooled, width), BF),
            pltpu.VMEM((half, width), BF),
            pltpu.VMEM((rows, width), F32),
            pltpu.VMEM((half - rows, width), BF),
            pltpu.SemaphoreType.DMA((12,)),
        ],
        flops=unit_flops, nbytes=6 * 2**20, vmem=60.5,
    )
    got = near_reduce(rest.reshape(-1, rows, width))
    (grad_images,) = local(finish_kernel, [((rows, width), F32, VMEM)], [scal, images, own] + got, smem=1)
    (grad_texts,) = local(
        finish_texts_kernel, [((rows, width), F32, HBM)], [scal, texts, dyr], smem=1,
        scratch=[pltpu.VMEM((rows, width), F32), pltpu.SemaphoreType.DMA((4,))],
    )
    return (grad_images, grad_texts)


def solution(mesh):
    fine = Mesh(mesh.devices.reshape(2, 4, 2, 2, 8), AXES)
    split = P(AXES, None)
    return jax.shard_map(
        on_device,
        mesh=fine,
        in_specs=(split, split, P(), P()),
        out_specs=(split, split),
        check_vma=False,
    )
```

```python
import jax
import jax.numpy as jnp
from jax import lax
from jax.experimental import pallas as pl
from jax.experimental.pallas import tpu as pltpu
from jax.sharding import Mesh, PartitionSpec as P

AXES = ("yh", "x", "core", "yl", "z")
PLANE = ("yh", "x", "yl")
BF = jnp.bfloat16
F32 = jnp.float32
LOG2E = 1.4426950408889634
ROWS = 64
NT = (((1,), (1,)), ((), ()))
TN = (((0,), (0,)), ((), ()))


def shifted(block, axis, distance):
    n = lax.axis_size(axis)
    return lax.ppermute(block, axis, [(i, (i + distance) % n) for i in range(n)])


def to_unit(raw):
    norm = jnp.sqrt(jnp.sum(raw * raw, axis=1, keepdims=True) + 1e-06)
    return (raw / norm, norm)


def from_unit(grad, unit, norm):
    return (grad - unit * jnp.sum(unit * grad, axis=1, keepdims=True)) / norm


def unit_rows(raw):
    norm = jnp.sqrt(jnp.sum(raw * raw, axis=1, keepdims=True) + 1e-06)
    return (raw / norm).astype(BF)


def spread_kernel(raw, out, unit, sems):
    unit[...] = unit_rows(raw[...])
    copies = [pltpu.make_async_copy(unit, out.at[k], sems.at[k]) for k in range(out.shape[0])]
    for copy in copies:
        copy.start()
    for copy in copies:
        copy.wait()


def unit_kernel(raw, out):
    out[...] = unit_rows(raw[...])


def pack_kernel(*refs):
    for k, block in enumerate(refs[:-1]):
        refs[-1][k * ROWS : (k + 1) * ROWS] = block[...]


def sigmoid(temp, offset, dots):
    return 1.0 / (1.0 + jnp.exp2(dots * (temp * -LOG2E) + offset * -LOG2E))


def pair_kernel(place, scal, xs, xo, ts, dxs, dxo, dy, x, held, mine, theirs, part, sems):
    temp = scal[0]
    offset = scal[1]
    half = xs.shape[0]
    pooled = ts.shape[0]
    wide = 512
    step = 256
    loads = [
        pltpu.make_async_copy(xs, x.at[0:half], sems.at[0]),
        pltpu.make_async_copy(xo, x.at[half : 2 * half], sems.at[1]),
    ]
    for copy in loads:
        copy.start()
    for h, copy in enumerate(loads):
        copy.wait()
        cols = slice(h * half, (h + 1) * half)
        for j in range(pooled // step):
            sl = pl.ds(j * step, step)
            dots = lax.dot_general(ts[sl], x[cols], NT, preferred_element_type=F32)
            held[sl, cols] = sigmoid(temp, offset, dots).astype(BF)
    at = pl.multiple_of(place[0] * ROWS, ROWS)
    dots = lax.dot_general(ts[pl.ds(at, ROWS)], x[0:ROWS], NT, preferred_element_type=F32)
    eye = lax.broadcasted_iota(jnp.int32, (ROWS, ROWS), 0) == lax.broadcasted_iota(
        jnp.int32, (ROWS, ROWS), 1
    )
    held[pl.ds(at, ROWS), 0:ROWS] = (sigmoid(temp, offset, dots) - eye.astype(F32)).astype(BF)
    copies = []

    def send(src, dst):
        copies.append(pltpu.make_async_copy(src, dst, sems.at[2 + len(copies)]))
        copies[-1].start()

    for h, (buf, out) in enumerate(((mine, dxs), (theirs, dxo))):
        for i in range(0, half, wide):
            cols = slice(h * half + i, h * half + i + wide)
            dots = lax.dot_general(held[:, cols], ts[...], TN, preferred_element_type=F32)
            buf[i : i + wide] = dots.astype(buf.dtype)
            send(buf.at[i : i + wide], out.at[i : i + wide])
    for j in range(0, pooled, step):
        part[j : j + step] = jnp.dot(held[j : j + step], x[...], preferred_element_type=F32).astype(BF)
        send(part.at[j : j + step], dy.at[j : j + step])
    for copy in copies:
        copy.wait()


def join_kernel(dxs, other, own, rest):
    own[...] = dxs[0:ROWS] + other[0:ROWS].astype(F32)
    rest[...] = (dxs[ROWS:] + other[ROWS:].astype(F32)).astype(BF)


VMEM = pl.BlockSpec(memory_space=pltpu.VMEM)
SMEM = pl.BlockSpec(memory_space=pltpu.SMEM)
HBM = pl.BlockSpec(memory_space=pltpu.HBM)


def local(kernel, outs, args, smem=0, hbm=0, scratch=(), flops=0, nbytes=2**20, trans=0, vmem=8):
    specs = [SMEM] * smem + [HBM] * hbm
    return pl.pallas_call(
        kernel,
        out_shape=tuple((pltpu.HBM if spec is HBM else jax.ShapeDtypeStruct)(shape, dtype) for shape, dtype, spec in outs),
        in_specs=specs + [VMEM] * (len(args) - len(specs)),
        out_specs=tuple(spec for _, _, spec in outs),
        scratch_shapes=list(scratch),
        compiler_params=pltpu.CompilerParams(vmem_limit_bytes=vmem * 2**20),
        cost_estimate=pl.CostEstimate(flops=flops, bytes_accessed=nbytes, transcendentals=trans),
    )(*args)


def add(a, b):
    return (a.astype(F32) + b.astype(F32)).astype(BF)


def ring_gather(block):
    far = shifted(block, "z", 4)
    up = [block]
    down = [block]
    for _ in range(3):
        up.append(shifted(up[-1], "z", -1))
        down.append(shifted(down[-1], "z", 1))
    return up + [far] + down[:0:-1]


def near_reduce(rest):
    direct = [shifted(rest[k - 1], "z", k) for k in (4, 3, 5)]
    up, down = shifted(rest[1], "z", 1), shifted(rest[5], "z", -1)
    up, down = shifted(add(rest[0], up), "z", 1), shifted(add(rest[6], down), "z", -1)
    return direct + [up, down]


def on_device(images, texts, log_temp, bias):
    temp = jnp.exp(log_temp[0])
    rows, width = images.shape
    n_plane = lax.axis_size(PLANE)
    half = ROWS * lax.axis_size("z")
    pooled = ROWS * n_plane
    (spread,) = local(
        spread_kernel, [((n_plane, rows, width), BF, HBM)], [texts],
        scratch=[pltpu.VMEM((rows, width), BF), pltpu.SemaphoreType.DMA((n_plane,))],
    )
    spread, images = lax.optimization_barrier((spread, images))
    ts = lax.all_to_all(spread, PLANE, 0, 0, tiled=True).reshape(pooled, width)
    (x,) = local(unit_kernel, [((rows, width), BF, VMEM)], [images])
    (xs,) = local(pack_kernel, [((half, width), BF, VMEM)], ring_gather(x))
    xo = shifted(xs, "core", 1)
    place = lax.axis_index(PLANE).astype(jnp.int32).reshape(1)
    scal = jnp.stack([temp, bias[0]])
    unit_flops = 2 * half * pooled * width
    dxs, dxo, dy = local(
        pair_kernel,
        [((half, width), F32, HBM), ((half, width), BF, HBM), ((pooled, width), BF, HBM)],
        [place, scal, xs, xo, ts], smem=2, hbm=2,
        scratch=[
            pltpu.VMEM((2 * half, width), BF),
            pltpu.VMEM((pooled, 2 * half), BF),
            pltpu.VMEM((half, width), F32),
            pltpu.VMEM((half, width), BF),
            pltpu.VMEM((pooled, width), BF),
            pltpu.SemaphoreType.DMA((8,)),
        ],
        flops=6 * unit_flops, nbytes=9 * 2**20, trans=4 * half * pooled, vmem=24,
    )
    dyr = lax.all_to_all(dy.reshape(n_plane, rows, width), PLANE, 0, 0, tiled=True)
    other = shifted(dxo, "core", 1)
    own, rest = local(
        join_kernel, [((rows, width), F32, VMEM), ((half - rows, width), BF, VMEM)], [dxs, other],
        nbytes=5 * 2**20, vmem=16,
    )
    got = near_reduce(rest.reshape(-1, rows, width))
    for part in got:
        own = own + part.astype(F32)
    grad_images = from_unit(temp * own, *to_unit(images))
    text_sum = jnp.sum(dyr.astype(F32), axis=0)
    grad_texts = from_unit(temp * text_sum, *to_unit(texts))
    return (grad_images, grad_texts)


def solution(mesh):
    fine = Mesh(mesh.devices.reshape(2, 4, 2, 2, 8), AXES)
    split = P(AXES, None)
    return jax.shard_map(
        on_device,
        mesh=fine,
        in_specs=(split, split, P(), P()),
        out_specs=(split, split),
        check_vma=False,
    )
```

```python
import jax
import jax.numpy as jnp
from jax import lax
from jax.experimental import pallas as pl
from jax.experimental.pallas import tpu as pltpu
from jax.sharding import Mesh, PartitionSpec as P

AXES = ("yh", "x", "core", "yl", "z")
PLANE = ("yh", "x", "yl")
BF = jnp.bfloat16
F32 = jnp.float32
LOG2E = 1.4426950408889634
ROWS = 64
NT = (((1,), (1,)), ((), ()))
TN = (((0,), (0,)), ((), ()))


def shifted(block, axis, distance):
    n = lax.axis_size(axis)
    return lax.ppermute(block, axis, [(i, (i + distance) % n) for i in range(n)])


def to_unit(raw):
    norm = jnp.sqrt(jnp.sum(raw * raw, axis=1, keepdims=True) + 1e-06)
    return (raw / norm, norm)


def from_unit(grad, unit, norm):
    return (grad - unit * jnp.sum(unit * grad, axis=1, keepdims=True)) / norm


def unit_rows(raw):
    norm = jnp.sqrt(jnp.sum(raw * raw, axis=1, keepdims=True) + 1e-06)
    return (raw / norm).astype(BF)


def spread_kernel(raw, out, unit, sems):
    unit[...] = unit_rows(raw[...])
    copies = [pltpu.make_async_copy(unit, out.at[k], sems.at[k]) for k in range(out.shape[0])]
    for copy in copies:
        copy.start()
    for copy in copies:
        copy.wait()


def unit_kernel(raw, out):
    out[...] = unit_rows(raw[...])


def pack_kernel(*refs):
    for k, block in enumerate(refs[:-1]):
        refs[-1][k * ROWS : (k + 1) * ROWS] = block[...]


def sigmoid(temp, offset, dots):
    return 1.0 / (1.0 + jnp.exp2(dots * (temp * -LOG2E) + offset * -LOG2E))


def pair_kernel(place, scal, xs, xo, ts, dxs, dxo, dy, x, held, mine, theirs, part, sems):
    temp = scal[0]
    offset = scal[1]
    half = xs.shape[0]
    pooled = ts.shape[0]
    wide = 512
    step = 256
    loads = [
        pltpu.make_async_copy(xs, x.at[0:half], sems.at[0]),
        pltpu.make_async_copy(xo, x.at[half : 2 * half], sems.at[1]),
    ]
    for copy in loads:
        copy.start()
    for h, copy in enumerate(loads):
        copy.wait()
        cols = slice(h * half, (h + 1) * half)
        for j in range(pooled // step):
            sl = pl.ds(j * step, step)
            dots = lax.dot_general(ts[sl], x[cols], NT, preferred_element_type=F32)
            held[sl, cols] = sigmoid(temp, offset, dots).astype(BF)
    at = pl.multiple_of(place[0] * ROWS, ROWS)
    dots = lax.dot_general(ts[pl.ds(at, ROWS)], x[0:ROWS], NT, preferred_element_type=F32)
    eye = lax.broadcasted_iota(jnp.int32, (ROWS, ROWS), 0) == lax.broadcasted_iota(
        jnp.int32, (ROWS, ROWS), 1
    )
    held[pl.ds(at, ROWS), 0:ROWS] = (sigmoid(temp, offset, dots) - eye.astype(F32)).astype(BF)
    copies = []

    def send(src, dst):
        copies.append(pltpu.make_async_copy(src, dst, sems.at[2 + len(copies)]))
        copies[-1].start()

    for h, (buf, out) in enumerate(((mine, dxs), (theirs, dxo))):
        for i in range(0, half, wide):
            cols = slice(h * half + i, h * half + i + wide)
            dots = lax.dot_general(held[:, cols], ts[...], TN, preferred_element_type=F32)
            buf[i : i + wide] = dots.astype(buf.dtype)
            send(buf.at[i : i + wide], out.at[i : i + wide])
    for j in range(0, pooled, step):
        part[j : j + step] = jnp.dot(held[j : j + step], x[...], preferred_element_type=F32).astype(BF)
        send(part.at[j : j + step], dy.at[j : j + step])
    for copy in copies:
        copy.wait()


def join_kernel(dxs, other, own, rest):
    own[...] = dxs[0:ROWS] + other[0:ROWS].astype(F32)
    rest[...] = (dxs[ROWS:] + other[ROWS:].astype(F32)).astype(BF)


def finish_texts_kernel(scal, raw, got, out):
    total = got[0].astype(F32)
    for k in range(1, got.shape[0]):
        total += got[k].astype(F32)
    unit, norm = to_unit(raw[...])
    out[...] = from_unit(scal[0] * total, unit, norm)


VMEM = pl.BlockSpec(memory_space=pltpu.VMEM)
SMEM = pl.BlockSpec(memory_space=pltpu.SMEM)
HBM = pl.BlockSpec(memory_space=pltpu.HBM)


def local(kernel, outs, args, smem=0, hbm=0, scratch=(), flops=0, nbytes=2**20, trans=0, vmem=8):
    specs = [SMEM] * smem + [HBM] * hbm
    return pl.pallas_call(
        kernel,
        out_shape=tuple((pltpu.HBM if spec is HBM else jax.ShapeDtypeStruct)(shape, dtype) for shape, dtype, spec in outs),
        in_specs=specs + [VMEM] * (len(args) - len(specs)),
        out_specs=tuple(spec for _, _, spec in outs),
        scratch_shapes=list(scratch),
        compiler_params=pltpu.CompilerParams(vmem_limit_bytes=vmem * 2**20),
        cost_estimate=pl.CostEstimate(flops=flops, bytes_accessed=nbytes, transcendentals=trans),
    )(*args)


def add(a, b):
    return (a.astype(F32) + b.astype(F32)).astype(BF)


def ring_gather(block):
    far = shifted(block, "z", 4)
    up = [block]
    down = [block]
    for _ in range(3):
        up.append(shifted(up[-1], "z", -1))
        down.append(shifted(down[-1], "z", 1))
    return up + [far] + down[:0:-1]


def near_reduce(rest):
    direct = [shifted(rest[k - 1], "z", k) for k in (4, 3, 5)]
    up, down = shifted(rest[1], "z", 1), shifted(rest[5], "z", -1)
    up, down = shifted(add(rest[0], up), "z", 1), shifted(add(rest[6], down), "z", -1)
    return direct + [up, down]


def on_device(images, texts, log_temp, bias):
    temp = jnp.exp(log_temp[0])
    rows, width = images.shape
    n_plane = lax.axis_size(PLANE)
    half = ROWS * lax.axis_size("z")
    pooled = ROWS * n_plane
    (spread,) = local(
        spread_kernel, [((n_plane, rows, width), BF, HBM)], [texts],
        scratch=[pltpu.VMEM((rows, width), BF), pltpu.SemaphoreType.DMA((n_plane,))],
    )
    spread, images = lax.optimization_barrier((spread, images))
    ts = lax.all_to_all(spread, PLANE, 0, 0, tiled=True).reshape(pooled, width)
    (x,) = local(unit_kernel, [((rows, width), BF, VMEM)], [images])
    (xs,) = local(pack_kernel, [((half, width), BF, VMEM)], ring_gather(x))
    xo = shifted(xs, "core", 1)
    place = lax.axis_index(PLANE).astype(jnp.int32).reshape(1)
    scal = jnp.stack([temp, bias[0]])
    unit_flops = 2 * half * pooled * width
    dxs, dxo, dy = local(
        pair_kernel,
        [((half, width), F32, HBM), ((half, width), BF, HBM), ((pooled, width), BF, HBM)],
        [place, scal, xs, xo, ts], smem=2, hbm=2,
        scratch=[
            pltpu.VMEM((2 * half, width), BF),
            pltpu.VMEM((pooled, 2 * half), BF),
            pltpu.VMEM((half, width), F32),
            pltpu.VMEM((half, width), BF),
            pltpu.VMEM((pooled, width), BF),
            pltpu.SemaphoreType.DMA((8,)),
        ],
        flops=6 * unit_flops, nbytes=9 * 2**20, trans=4 * half * pooled, vmem=24,
    )
    dyr = lax.all_to_all(dy.reshape(n_plane, rows, width), PLANE, 0, 0, tiled=True)
    other = shifted(dxo, "core", 1)
    own, rest = local(
        join_kernel, [((rows, width), F32, VMEM), ((half - rows, width), BF, VMEM)], [dxs, other],
        nbytes=5 * 2**20, vmem=16,
    )
    got = near_reduce(rest.reshape(-1, rows, width))
    for part in got:
        own = own + part.astype(F32)
    grad_images = from_unit(temp * own, *to_unit(images))
    (grad_texts,) = local(finish_texts_kernel, [((rows, width), F32, VMEM)], [scal, texts, dyr], smem=1)
    return (grad_images, grad_texts)


def solution(mesh):
    fine = Mesh(mesh.devices.reshape(2, 4, 2, 2, 8), AXES)
    split = P(AXES, None)
    return jax.shard_map(
        on_device,
        mesh=fine,
        in_specs=(split, split, P(), P()),
        out_specs=(split, split),
        check_vma=False,
    )
```
